256 devices in a mesh: dp: 16 (over z_hi, x), expert: 16 (over y, z_lo, core).
Axes of the slice: x: 4, y: 4, z: 8 (z_hi: 4, z_lo: 2; z = z_hi * 2 + z_lo), core: 2. Of those that a mesh axis runs over, the one named last changes fastest.
Arguments:
- tokens: bfloat16 [2048, 3072], P('dp'), may hold values from -6 to 6
- cotangent: bfloat16 [2048, 3072], P('dp'), may hold values from -6 to 6
- routes: int32 [2048, 4], P('dp'), may hold values from 0 to 15, all different within a row; in each aligned block of 128 rows (0 to 127, 128 to 255, ...) at most 48 rows name the same one
- route_weights: float32 [2048, 4], P('dp'), may hold values from 0.1 to 0.6
- gate_weight: bfloat16 [16, 3072, 6144], P('expert', None, 'dp'), may hold values from -0.109375 to 0.109375
- down_weight: bfloat16 [16, 6144, 3072], P('expert', 'dp'), may hold values from -0.078125 to 0.078125
Outputs:
- mixed: bfloat16 [2048, 3072], P('dp')
- token_grad: bfloat16 [2048, 3072], P('dp')
- gate_grad: bfloat16 [16, 3072, 6144], P('expert', None, 'dp')
- down_grad: bfloat16 [16, 6144, 3072], P('expert', 'dp')
The draws below stay inside these ranges and needn't reach their ends.
Inputs may be any that keep to these rules, and one draw needn't show every extreme that they name: `routes`: each row names 4 different experts. In each aligned block of 128 rows no expert is named by more than 48 rows, and in every draw some expert is named by exactly 48 rows of some block.
All inputs are finite; a program needn't handle non-finite values.
Results may differ from the reference program's by a relative error of at most 0.022.
Values may be sent and summed in bfloat16 or wider, within the bound.
A program may use at most 128 MiB of HBM per device.

```python
import math
import jax
import jax.numpy as jnp
import numpy as np
from jax import lax

D = 3072
FF = 6144
EXPERTS = 16
TOP = 4
TOK_DEV = 128
CAP = 48
TOKENS = 2048
N_DP = 16


def steps_of(own_key, dims, split, low, top_value):
    factor_of = 1.0
    for dim, shards_of in split:
        heights = jax.random.uniform(jax.random.fold_in(jax.random.fold_in(own_key, 6), dim), (shards_of,), jnp.float32, low / len(split), top_value / len(split))
        factor_of = factor_of * jnp.repeat(jnp.exp(heights), dims[dim] // shards_of).reshape((-1,) + (1,) * (len(dims) - 1 - dim))
    return factor_of


def routed_block(stream_key, own, number, rows, number_of, top, most, skew):
    sequence = jax.random.permutation(stream_key, number_of)
    heavy_load, common = shares(number_of, rows * top, most, skew, True), shares(number_of, rows * top, most, skew, False)
    places = jnp.arange(number_of)

    def named(sizes, offset_by):
        used = int((sizes > 0).sum())
        fixed = max(1, used // 4)
        passed = fixed + (places - fixed + offset_by * (used - fixed)) % max(1, number_of - fixed)
        return jnp.zeros((number_of,), jnp.int32).at[sequence[jnp.where(places < fixed, places, passed)]].set(jnp.asarray(sizes, jnp.int32))

    sizes = jnp.where(number % 4 == 0, named(heavy_load, number // 4), named(common, number - number // 4 - 1))
    mixed = jax.random.permutation(jax.random.fold_in(own, 3), number_of)
    source_of, sink = mixed[0:number_of // 2 * 2:2], mixed[1:number_of // 2 * 2:2]
    room = jnp.minimum(sizes[source_of] - 1, most - sizes[sink]) // 2
    room = jnp.where((source_of == sequence[0]) | (sink == sequence[0]) | (sizes[sink] == 0), 0, jnp.maximum(room, 0))
    passed = jax.random.randint(jax.random.fold_in(own, 4), (number_of // 2,), 0, 1 << 20) % (room + 1)
    sizes = sizes.at[source_of].add(-passed).at[sink].add(passed)
    items = jnp.searchsorted(jnp.cumsum(sizes), jnp.arange(rows * top), side="right").astype(jnp.int32)
    grid = items.reshape(top, rows).T
    grid = grid[jax.random.permutation(jax.random.fold_in(own, 1), rows)]
    offset_by = jax.random.randint(jax.random.fold_in(own, 2), (rows, 1), 0, top)
    return jnp.take_along_axis(grid, (jnp.arange(top)[None, :] + offset_by) % top, axis=1)


def shares(count, total, bound, lean, full):
    loads = [(1 << 20) // math.isqrt(rank ** lean) + 1 for rank in range(1, count + 1)]
    largest = bound if full else min(bound, max(-(-total // count), total * loads[0] // sum(loads)))
    least = 1 if total - largest >= count - 1 else 0
    given, spare = [largest] + [least] * (count - 1), total - largest - least * (count - 1)
    while spare > 0:
        movable = [i for i in range(1, count) if given[i] < largest] or [i for i in range(1, count) if given[i] < bound]
        whole, left = sum([loads[i] for i in movable]), spare
        for i in movable:
            more = min(bound - given[i], max(1, left * loads[i] // whole), spare)
            given[i] = given[i] + more
            spare = spare - more
    return np.array(given)


def bell_draw(rng, dims, scale, bound, pieces=(), held_as=jnp.bfloat16):
    gain = steps_of(rng, dims, pieces, -0.22, 0.18) if pieces else 1.0
    entries = jax.random.normal(rng, dims, jnp.float32) * scale * gain
    return jnp.minimum(jnp.maximum(entries, -bound), bound).astype(held_as)


def setup_inputs(seed: int = 0) -> dict:
    key_list = jax.random.split(jax.random.key(seed), 7)
    tokens = bell_draw(key_list[0], (TOKENS, D), 1.0, 6.0, ((0, 16),))
    cotangent = bell_draw(key_list[1], (TOKENS, D), 1.0, 6.0, ((0, 16),))
    routes_keys = jax.random.split(jax.random.fold_in(key_list[2], 1), TOKENS // TOK_DEV)
    routes_turns = jax.random.permutation(jax.random.fold_in(key_list[2], 3), TOKENS // TOK_DEV)
    routes = jax.vmap(lambda own, number: routed_block(jax.random.fold_in(key_list[2], 2), own, number, TOK_DEV, EXPERTS, TOP, CAP, 2))(routes_keys, routes_turns).reshape((TOKENS, TOP))
    route_weights = jnp.clip(0.1 + 0.5 * jax.random.uniform(key_list[3], (TOKENS, TOP), jnp.float32) ** steps_of(key_list[3], (TOKENS, TOP), ((0, 16),), -0.2, 0.2), 0.1, 0.6)
    gate_weight = bell_draw(key_list[4], (EXPERTS, D, FF), D ** -0.5, 0.109375, ((0, 16), (2, 16)))
    down_weight = bell_draw(key_list[5], (EXPERTS, FF, D), FF ** -0.5, 0.078125, ((0, 16), (1, 16)))
    return {"tokens": tokens, "cotangent": cotangent, "routes": routes, "route_weights": route_weights, "gate_weight": gate_weight, "down_weight": down_weight}


def grouped_round(left, right, form):
    parts = jnp.einsum(form, left.astype(jnp.float32), right.astype(jnp.float32), precision=lax.Precision.HIGHEST)
    rounded = lax.optimization_barrier(parts.astype(jnp.bfloat16))
    return jnp.sum(rounded.astype(jnp.float32), axis=0)


def one_expert(operands):
    token_rows, grad_rows, gate, down = operands
    shard = FF // N_DP
    pre_act = jnp.dot(token_rows, gate, preferred_element_type=jnp.float32)
    act_rows = jax.nn.silu(pre_act).astype(jnp.bfloat16)
    expert_out = grouped_round(act_rows.reshape(-1, N_DP, shard), down.reshape(N_DP, shard, D), 'rsf,sfd->srd')
    back_act = jnp.dot(grad_rows, down.T, preferred_element_type=jnp.float32)
    sigma = jax.nn.sigmoid(pre_act)
    grad_pre = (back_act * sigma * (1.0 + pre_act * (1.0 - sigma))).astype(jnp.bfloat16)
    down_grad = jnp.dot(act_rows.T, grad_rows, preferred_element_type=jnp.float32).astype(jnp.bfloat16)
    gate_grad = jnp.dot(token_rows.T, grad_pre, preferred_element_type=jnp.float32).astype(jnp.bfloat16)
    expert_back = grouped_round(grad_pre.reshape(-1, N_DP, shard), gate.reshape(D, N_DP, shard), 'rsf,dsf->srd')
    return expert_out, expert_back, gate_grad, down_grad


def reference(tokens, cotangent, routes, route_weights, gate_weight, down_weight):
    blocks = routes.reshape(N_DP, TOK_DEV, TOP)
    probs = route_weights.reshape(N_DP, TOK_DEV, TOP)
    expert_ids = jnp.arange(EXPERTS, dtype=jnp.int32)
    matches = blocks[:, None, :, :] == expert_ids[None, :, None, None]
    member = jnp.any(matches, axis=3)
    weight_sum = jnp.sum(jnp.where(matches, probs[:, None, :, :], 0.0), axis=3)
    position = jnp.cumsum(member.astype(jnp.int32), axis=2) - 1
    slots = jnp.arange(CAP, dtype=jnp.int32)
    selector = (member[:, :, None, :] & (position[:, :, None, :] == slots[None, None, :, None])).astype(jnp.float32)
    scale = jnp.einsum('bect,bet->ebc', selector, weight_sum, precision=lax.Precision.HIGHEST)
    token_blocks = tokens.reshape(N_DP, TOK_DEV, D).astype(jnp.float32)
    grad_blocks = cotangent.reshape(N_DP, TOK_DEV, D).astype(jnp.float32)
    token_rows = jnp.einsum('bect,btd->ebcd', selector, token_blocks, precision=lax.Precision.HIGHEST)
    token_rows = token_rows.astype(jnp.bfloat16).reshape(EXPERTS, N_DP * CAP, D)
    grad_rows = jnp.einsum('bect,btd->ebcd', selector, grad_blocks, precision=lax.Precision.HIGHEST) * scale[..., None]
    grad_rows = grad_rows.astype(jnp.bfloat16).reshape(EXPERTS, N_DP * CAP, D)
    expert_out, expert_back, gate_grad, down_grad = lax.map(one_expert, (token_rows, grad_rows, gate_weight, down_weight))
    expert_out = expert_out.reshape(EXPERTS, N_DP, CAP, D) * scale[..., None]
    expert_back = expert_back.reshape(EXPERTS, N_DP, CAP, D)
    mixed = jnp.einsum('bect,ebcd->btd', selector, expert_out, precision=lax.Precision.HIGHEST)
    token_grad = jnp.einsum('bect,ebcd->btd', selector, expert_back, precision=lax.Precision.HIGHEST)
    mixed = mixed.reshape(TOKENS, D).astype(jnp.bfloat16)
    token_grad = token_grad.reshape(TOKENS, D).astype(jnp.bfloat16)
    return mixed, token_grad, gate_grad, down_grad
```

```python
import functools

import jax
import jax.numpy as jnp
from jax import lax
from jax.experimental import pallas as pl
from jax.experimental.pallas import tpu as pltpu
from jax.sharding import PartitionSpec as P

MESH = pl.DeviceIdType.MESH
BF = jnp.bfloat16
F32 = jnp.float32
CAP = 48
TOK = 128
D = 3072
HID = 384
NE = 16
A_COLS = 2432
CHUNKS = ((0, 1024), (1024, 2048), (2048, A_COLS))
NCH = 3
VM = pl.BlockSpec(memory_space=pltpu.VMEM)
HB = pl.BlockSpec(memory_space=pl.ANY)


def kernel(
    tok, cot, routes, wts, gate_in, down_in,
    out, gg_out, dg_out,
    gat, par, rd1, rd2, gate, down, gg, dg, act_s, gp_s, ex, rx, ox, sel_s, scale_s,
    ssem, rsem, xs, xr, os_, or_, lsem,
):
    dp = lax.axis_index("dp")
    me = lax.axis_index("expert")
    h, x = dp // 4, dp % 4
    core, slot = me % 2, me // 2

    def peer(axis, step):
        if axis == "x":
            return (h * 4 + (x + step + 4) % 4, me)
        return (((h + step + 4) % 4) * 4 + x, me)

    load_gate = pltpu.make_async_copy(gate_in, gate, lsem.at[0])
    load_down = pltpu.make_async_copy(down_in, down, lsem.at[1])
    load_gate.start()
    load_down.start()

    barrier = pltpu.get_barrier_semaphore()
    for axis in ("x", "z"):
        for step in (1, -1):
            pl.semaphore_signal(barrier, inc=1, device_id=peer(axis, step), device_id_type=MESH)

    def greet(i, carry):
        pl.semaphore_signal(barrier, inc=1, device_id=(dp, (me + i) % NE), device_id_type=MESH)
        return carry

    lax.fori_loop(1, NE, greet, 0)

    r = routes[...]
    w = wts[...]
    lane16 = lax.broadcasted_iota(jnp.int32, (TOK, NE), 1)
    member = jnp.zeros((TOK, NE), F32)
    for k in range(4):
        member = member + jnp.where(r[:, k : k + 1] == lane16, 1.0, 0.0)
    below = lax.broadcasted_iota(jnp.int32, (TOK, TOK), 0) > lax.broadcasted_iota(
        jnp.int32, (TOK, TOK), 1
    )
    pos = jnp.dot(
        jnp.where(below, 1.0, 0.0).astype(BF), member.astype(BF), preferred_element_type=F32
    )
    mine = jnp.where(lane16 == me, 1.0, 0.0)
    mem_e = jnp.sum(member * mine, axis=1, keepdims=True)
    pos_e = jnp.sum(pos * mine, axis=1, keepdims=True)
    w_e = jnp.zeros((TOK, 1), F32)
    for k in range(4):
        w_e = w_e + jnp.where(r[:, k : k + 1] == me, w[:, k : k + 1], 0.0)
    lane = lax.broadcasted_iota(jnp.int32, (TOK, TOK), 1).astype(F32)
    sel_t = jnp.where((pos_e == lane) & (mem_e > 0.5), 1.0, 0.0)
    sel = sel_t.T[:CAP]
    w_row = jnp.broadcast_to(w_e, (TOK, TOK)).T[:CAP]
    scale_s[...] = jnp.broadcast_to(jnp.sum(sel * w_row, axis=1, keepdims=True), (CAP, 128))
    sel_b = sel.astype(BF)
    gat[0, 0, 0] = jnp.dot(sel_b, tok[...], preferred_element_type=F32).astype(BF)
    scaled = (cot[...].astype(F32) * w_e).astype(BF)
    gat[0, 0, 1] = jnp.dot(sel_b, scaled, preferred_element_type=F32).astype(BF)

    pl.semaphore_wait(barrier, 4 + NE - 1)

    started = []
    count = [0]

    def remote(src, dst, device):
        i = count[0]
        count[0] += 1
        copy = pltpu.make_async_remote_copy(
            src_ref=src, dst_ref=dst, send_sem=ssem.at[i], recv_sem=rsem.at[i],
            device_id=device, device_id_type=MESH,
        )
        return copy

    def go(copy):
        copy.start()
        started.append(copy)

    class Gather:
        def __init__(self, axis, at):
            self.plus, self.minus = peer(axis, 1), peer(axis, -1)
            self.at = at
            self.p, self.m, self.f = {}, {}, {}
            for arr in (0, 1):
                self.p[arr] = remote(at(0, arr), at(3, arr), self.plus)
                self.m[arr] = remote(at(0, arr), at(1, arr), self.minus)
            self.f[0] = remote(at(3, 0), at(2, 0), self.plus)
            self.f[1] = remote(at(1, 1), at(2, 1), self.minus)

        def start(self, arr):
            first, second = (self.p, self.m) if arr == 0 else (self.m, self.p)
            go(first[arr])
            go(second[arr])

        def fwd(self, arr):
            (self.p if arr == 0 else self.m)[arr].wait_recv()
            go(self.f[arr])

        def near(self, arr):
            (self.m if arr == 0 else self.p)[arr].wait_recv()

        def far(self, arr):
            self.f[arr].wait_recv()

    ca, cb = pl.ds(0, A_COLS), pl.ds(A_COLS, D - A_COLS)
    a1 = Gather("z", lambda i, arr: gat.at[i, 0, arr, :, ca])
    b1 = Gather("x", lambda i, arr: gat.at[0, i, arr, :, cb])
    a2 = [Gather("x", functools.partial(lambda u, i, arr: gat.at[u, i, arr, :, ca], u)) for u in range(4)]
    b2 = [Gather("z", functools.partial(lambda u, i, arr: gat.at[i, u, arr, :, cb], u)) for u in range(4)]

    def finish(ring):
        ring.near(0)
        ring.near(1)
        ring.far(0)
        ring.far(1)

    def rows(ref):
        return ref.reshape(4 * CAP, ref.shape[-1])

    def batch(u):
        t = rows(gat[u, :, 0])
        pre = jnp.dot(t, gate[...], preferred_element_type=F32)
        back = lax.dot_general(
            rows(gat[u, :, 1]), down[...], (((1,), (1,)), ((), ())), preferred_element_type=F32
        )
        s = jax.nn.sigmoid(pre)
        act = (pre * s).astype(BF)
        gp = (back * s * (1.0 + pre * (1.0 - s))).astype(BF)
        act_s[u] = act
        gp_s[u] = gp

        def cols(j, carry):
            c = pl.ds(pl.multiple_of(j * 512, 512), 512)
            o = jnp.dot(act_s[u], down[:, c], preferred_element_type=F32).astype(BF)
            par[u, :, 0, :, c] = o.reshape(4, CAP, 512)
            b = lax.dot_general(
                gp_s[u], gate[c, :], (((1,), (1,)), ((), ())), preferred_element_type=F32
            ).astype(BF)
            par[u, :, 1, :, c] = b.reshape(4, CAP, 512)
            return carry

        lax.fori_loop(0, D // 512, cols, 0)

    for arr in (0, 1):
        a1.start(arr)
    for arr in (0, 1):
        b1.start(arr)
    for arr in (0, 1):
        a2[0].start(arr)
        b2[0].start(arr)
    b1.fwd(0)
    b1.fwd(1)
    a2[0].fwd(0)
    a2[0].fwd(1)
    a1.fwd(0)
    a2[3].start(0)
    a1.fwd(1)
    a2[1].start(1)
    b1.near(0)
    b1.near(1)
    for arr in (0, 1):
        b2[1].start(arr)
        b2[3].start(arr)
    load_gate.wait()
    load_down.wait()
    finish(a2[0])
    b1.far(0)
    b1.far(1)
    for arr in (0, 1):
        b2[2].start(arr)
    batch(0)
    a1.near(0)
    a2[1].start(0)
    a1.near(1)
    a2[3].start(1)
    a2[3].fwd(0)
    a2[1].fwd(1)
    b2[0].fwd(0)
    b2[0].fwd(1)
    a1.far(0)
    a2[2].start(0)
    a1.far(1)
    a2[2].start(1)
    a2[1].fwd(0)
    a2[3].fwd(1)
    for u in (1, 3):
        b2[u].fwd(0)
        b2[u].fwd(1)
    b2[2].fwd(0)
    b2[2].fwd(1)
    for u in range(4):
        b2[u].near(0)
        b2[u].near(1)
    finish(a2[1])
    batch(1)
    a2[2].fwd(0)
    a2[2].fwd(1)
    finish(a2[3])
    batch(3)
    for u in range(4):
        b2[u].far(0)
        b2[u].far(1)
    finish(a2[2])
    batch(2)

    class Reduce:
        def __init__(self, axis, at, land, c):
            plus, minus = peer(axis, 1), peer(axis, -1)
            self.at, self.land, self.c = at, land, c
            self.f0 = remote(at(2, 0), land(0, 0), plus)
            self.f1 = remote(at(2, 1), land(0, 1), minus)
            self.l1 = remote(at(1, 1), land(1, 1), plus)
            self.r0 = remote(at(3, 0), land(2, 0), minus)
            self.l0 = remote(at(1, 0), land(1, 0), plus)
            self.r1 = remote(at(3, 1), land(2, 1), minus)

        def start(self):
            go(self.f0)
            go(self.f1)
            go(self.l1)
            go(self.r0)

        def fwd(self):
            for f, copy, i, arr in ((self.f0, self.l0, 1, 0), (self.f1, self.r1, 3, 1)):
                f.wait_recv()
                dst = self.at(i, arr)
                dst[...] = (dst[...].astype(F32) + self.land(0, arr)[...].astype(F32)).astype(BF)
                go(copy)

        def total(self, arr):
            return (
                self.at(0, arr)[...].astype(F32)
                + self.land(1, arr)[...].astype(F32)
                + self.land(2, arr)[...].astype(F32)
            )

        def arrive(self):
            for copy in (self.l1, self.r0, self.l0, self.r1):
                copy.wait_recv()

        def fin(self):
            self.arrive()
            for arr in (0, 1):
                self.at(0, arr)[...] = self.total(arr).astype(BF)

    def stage1(axis, u, c):
        if axis == "x":
            at = lambda i, arr: par.at[u, i, arr, :, c]
        else:
            at = lambda i, arr: par.at[i, u, arr, :, c]
        return Reduce(axis, at, lambda kind, arr: rd1.at[u, kind, arr, :, c], c)

    def stage2(axis, c):
        if axis == "x":
            at = lambda i, arr: par.at[0, i, arr, :, c]
        else:
            at = lambda i, arr: par.at[i, 0, arr, :, c]
        return Reduce(axis, at, lambda kind, arr: rd2.at[kind, arr, :, c], c)

    order = (2, 1, 3, 0)
    first = [[stage1("x", u, pl.ds(lo, hi - lo)) for u in order] for lo, hi in CHUNKS]
    second = [stage2("z", pl.ds(lo, hi - lo)) for lo, hi in CHUNKS]
    first_b = [stage1("z", u, cb) for u in order]
    second_b = stage2("x", cb)

    def home(ring, lo, hi):
        ring.arrive()
        for arr in (0, 1):
            v = ring.total(arr)
            if arr == 0:
                v = v * scale_s[:, :1]
            v = v.astype(BF)
            for i in range((hi - lo) // 128):
                tile = lo // 128 + i
                ex[tile // 8, arr, tile % 8] = v[:, 128 * i : 128 * (i + 1)]

    def exchange(k, e_to, e_from):
        return pltpu.make_async_remote_copy(
            src_ref=ex.at[k, e_to % 2, e_to // 2], dst_ref=rx.at[k, e_from],
            send_sem=xs.at[k, e_to], recv_sem=xr.at[k, e_from],
            device_id=(dp, e_to), device_id_type=MESH,
        )

    def exchange_start(k):
        def one(i, carry):
            exchange(k, (me + i) % NE, me).start()
            return carry

        lax.fori_loop(1, NE, one, 0)
        rx[k, me] = ex[k, core, slot]

    def place(k, owner):
        return out.at[
            owner % 2, :, pl.ds(pl.multiple_of(k * 1024 + (owner // 2) * 128, 128), 128)
        ]

    def spread(k, e_to, e_from):
        return pltpu.make_async_remote_copy(
            src_ref=ox.at[k], dst_ref=place(k, e_from),
            send_sem=os_.at[k, e_to], recv_sem=or_.at[k, e_from],
            device_id=(dp, e_to), device_id_type=MESH,
        )

    def keep(k):
        return pltpu.make_async_copy(ox.at[k], place(k, me), lsem.at[4 + k])

    def exchange_finish(k):
        def one(i, carry):
            exchange(k, me, (me + i) % NE).wait_recv()
            return carry

        lax.fori_loop(1, NE, one, 0)
        ox[k] = jnp.dot(
            sel_s[...], rx[k].reshape(NE * CAP, 128), preferred_element_type=F32
        ).astype(BF)
        keep(k).start()

        def two(i, carry):
            spread(k, (me + i) % NE, me).start()
            return carry

        lax.fori_loop(1, NE, two, 0)

    def grads(j):
        c = pl.ds(512 * j, 512)
        t = gat[:, :, 0, :, c].reshape(NE * CAP, 512)
        g = gat[:, :, 1, :, c].reshape(NE * CAP, 512)
        dg[:, c] = lax.dot_general(
            act_s[...].reshape(NE * CAP, HID), g, (((0,), (0,)), ((), ())),
            preferred_element_type=F32,
        ).astype(BF)
        gg[c, :] = lax.dot_general(
            t, gp_s[...].reshape(NE * CAP, HID), (((0,), (0,)), ((), ())),
            preferred_element_type=F32,
        ).astype(BF)

    for ring in first[0]:
        ring.start()
    for ring in first_b:
        ring.start()

    lo = lax.broadcasted_iota(jnp.int32, (NE, NE * CAP), 0) * CAP
    j = lax.broadcasted_iota(jnp.int32, (NE, NE * CAP), 1)
    ours = (j >= lo) & (j < lo + CAP)
    within = jnp.sum(jnp.where(ours, j - lo, 0), axis=0, keepdims=True).astype(F32)
    spread_e = jnp.where(ours, 1.0, 0.0).astype(BF)
    mem_x = jnp.dot(member.astype(BF), spread_e, preferred_element_type=F32)
    pos_x = jnp.dot(pos.astype(BF), spread_e, preferred_element_type=F32)
    sel_s[...] = jnp.where((mem_x > 0.5) & (pos_x == within), 1.0, 0.0).astype(BF)

    for k in range(NCH):
        for i in range(4):
            first[k][i].fwd()
            if k == 0:
                grads(i)
                first_b[i].fwd()
            if k + 1 < NCH:
                first[k + 1][i].start()
        if k == 0:
            grads(4)
            grads(5)
            store_gg = pltpu.make_async_copy(gg, gg_out, lsem.at[2])
            store_dg = pltpu.make_async_copy(dg, dg_out, lsem.at[3])
            store_gg.start()
            store_dg.start()
        for i in range(4):
            first[k][i].fin()
        second[k].start()
        if k == 0:
            for i in range(4):
                first_b[i].fin()
            second_b.start()
        if k >= 1:
            lo_c, hi_c = CHUNKS[k - 1]
            if k == 1:
                second_b.fwd()
            home(second[k - 1], lo_c, hi_c)
            exchange_start(k - 1)
        if k >= 2:
            exchange_finish(k - 2)
        second[k].fwd()
    home(second_b, A_COLS, D)
    home(second[NCH - 1], *CHUNKS[NCH - 1])
    exchange_start(NCH - 1)
    exchange_finish(NCH - 2)
    exchange_finish(NCH - 1)

    store_gg.wait()
    store_dg.wait()
    for k in range(NCH):
        keep(k).wait()

        def last(i, carry, k=k):
            spread(k, me, (me + i) % NE).wait_recv()
            spread(k, (me + i) % NE, me).wait_send()
            exchange(k, (me + i) % NE, me).wait_send()
            return carry

        lax.fori_loop(1, NE, last, 0)
    for copy in started:
        copy.wait_send()


N_COPY = 10 * 6 + 20 * 6


def shards(tokens, cotangent, routes, route_weights, gate_weight, down_weight):
    gate_weight = gate_weight.reshape(D, HID)
    down_weight = down_weight.reshape(HID, D)
    out, gg, dg = pl.pallas_call(
        kernel,
        out_shape=(
            jax.ShapeDtypeStruct((2, TOK, D), BF),
            jax.ShapeDtypeStruct((D, HID), BF),
            jax.ShapeDtypeStruct((HID, D), BF),
        ),
        in_specs=[VM, VM, VM, VM, HB, HB],
        out_specs=(HB, HB, HB),
        scratch_shapes=[
            pltpu.VMEM((4, 4, 2, CAP, D), BF),
            pltpu.VMEM((4, 4, 2, CAP, D), BF),
            pltpu.VMEM((4, 3, 2, CAP, D), BF),
            pltpu.VMEM((3, 2, CAP, D), BF),
            pltpu.VMEM((D, HID), BF),
            pltpu.VMEM((HID, D), BF),
            pltpu.VMEM((D, HID), BF),
            pltpu.VMEM((HID, D), BF),
            pltpu.VMEM((4, 4 * CAP, HID), BF),
            pltpu.VMEM((4, 4 * CAP, HID), BF),
            pltpu.VMEM((NCH, 2, 8, CAP, 128), BF),
            pltpu.VMEM((NCH, NE, CAP, 128), BF),
            pltpu.VMEM((NCH, TOK, 128), BF),
            pltpu.VMEM((TOK, NE * CAP), BF),
            pltpu.VMEM((CAP, 128), F32),
            pltpu.SemaphoreType.DMA((N_COPY,)),
            pltpu.SemaphoreType.DMA((N_COPY,)),
            pltpu.SemaphoreType.DMA((NCH, NE)),
            pltpu.SemaphoreType.DMA((NCH, NE)),
            pltpu.SemaphoreType.DMA((NCH, NE)),
            pltpu.SemaphoreType.DMA((NCH, NE)),
            pltpu.SemaphoreType.DMA((4 + NCH,)),
        ],
        compiler_params=pltpu.CompilerParams(
            collective_id=0, has_side_effects=True, vmem_limit_bytes=56 * 2**20
        ),
        cost_estimate=pl.CostEstimate(
            flops=12 * 768 * D * HID, bytes_accessed=2 * 10**7, transcendentals=768 * HID
        ),
        name="moe",
    )(tokens, cotangent, routes, route_weights, gate_weight, down_weight)
    return out[0], out[1], gg.reshape(1, D, HID), dg.reshape(1, HID, D)


def solution(mesh):
    return jax.shard_map(
        shards,
        mesh=mesh,
        in_specs=(
            P("dp", None),
            P("dp", None),
            P("dp", None),
            P("dp", None),
            P("expert", None, "dp"),
            P("expert", "dp", None),
        ),
        out_specs=(P("dp", None), P("dp", None), P("expert", None, "dp"), P("expert", "dp", None)),
        check_vma=False,
    )
```

```python
import functools

import jax
import jax.numpy as jnp
from jax import lax
from jax.experimental import pallas as pl
from jax.experimental.pallas import tpu as pltpu
from jax.sharding import PartitionSpec as P

MESH = pl.DeviceIdType.MESH
POS = (0, 1, 3, 2)
BF = jnp.bfloat16
F32 = jnp.float32
CAP = 48
TOK = 128
D = 3072
HID = 384
NE = 16
RA = 2688
EDGES = (0, 512, 1024, 1536, 2048, 2432, 2688)
NCH = 3
VM = pl.BlockSpec(memory_space=pltpu.VMEM)
HB = pl.BlockSpec(memory_space=pl.ANY)


def kernel(
    tok_in, cot_in, routes, wts, gate_in, down_in,
    out, gg_out, dg_out,
    tok, cot, raw, twin, gat, par, rd1, rd2, gate, down, gg, dg, act_s, gp_s, ex, rx, full, sel_s, scale_s,
    ssem, rsem, xs, xr, os_, or_, ks, kr, ts, tr, lsem,
):
    dp = lax.axis_index("dp")
    me = lax.axis_index("expert")
    h, x = dp // 4, dp % 4
    core, slot = me % 2, me // 2
    y, z_lo = me // 4, slot % 2

    def peer(axis, step):
        if axis == "x":
            return (h * 4 + (x + step + 4) % 4, me)
        if axis == "y":
            return (dp, (((y + step + 4) % 4) * 2 + z_lo) * 2 + core)
        return (((h + step + 4) % 4) * 4 + x, me)

    load_tok = pltpu.make_async_copy(tok_in, tok, lsem.at[4])
    load_cot = pltpu.make_async_copy(cot_in, cot, lsem.at[5])
    load_gate = pltpu.make_async_copy(gate_in, gate, lsem.at[0])
    load_down = pltpu.make_async_copy(down_in, down, lsem.at[1])
    half = pl.multiple_of(core * (D // 2), 128)
    load_raw = pltpu.make_async_copy(
        tok_in.at[:, pl.ds(pl.multiple_of(half + y * 384, 128), 384)],
        raw.at[0, 0, 0, pl.ds(0, TOK)],
        lsem.at[6 + 2 * NCH],
    )
    load_raw.start()
    load_tok.start()
    load_cot.start()
    load_gate.start()
    load_down.start()

    barrier = pltpu.get_barrier_semaphore()
    for axis in ("x", "z"):
        for step in (1, -1):
            pl.semaphore_signal(barrier, inc=1, device_id=peer(axis, step), device_id_type=MESH)

    def greet(i, carry):
        pl.semaphore_signal(barrier, inc=1, device_id=(dp, (me + i) % NE), device_id_type=MESH)
        return carry

    lax.fori_loop(1, NE, greet, 0)

    r = routes[...]
    w = wts[...]
    row16 = lax.broadcasted_iota(jnp.int32, (NE, TOK), 0)
    member = jnp.zeros((NE, TOK), F32)
    w_e = jnp.zeros((1, TOK), F32)
    for k in range(4):
        member = member + jnp.where(r[k : k + 1] == row16, 1.0, 0.0)
        w_e = w_e + jnp.where(r[k : k + 1] == me, w[k : k + 1], 0.0)
    before = lax.broadcasted_iota(jnp.int32, (TOK, TOK), 0) < lax.broadcasted_iota(
        jnp.int32, (TOK, TOK), 1
    )
    pos = jnp.dot(
        member.astype(BF), jnp.where(before, 1.0, 0.0).astype(BF), preferred_element_type=F32
    )
    slots = lax.broadcasted_iota(jnp.int32, (CAP, TOK), 0).astype(F32)

    def select(expert):
        mine = jnp.where(row16 == expert, 1.0, 0.0)
        mem_e = jnp.sum(member * mine, axis=0, keepdims=True)
        pos_e = jnp.sum(pos * mine, axis=0, keepdims=True)
        return jnp.where((pos_e == slots) & (mem_e > 0.5), 1.0, 0.0)

    sel = select(me)
    scale = jnp.sum(sel * w_e, axis=1, keepdims=True)
    scale_s[...] = jnp.broadcast_to(scale, (CAP, 128))
    sel_b = sel.astype(BF)
    pair = jnp.concatenate([sel, select(slot * 2 + 1 - core)], axis=0).astype(BF)
    for i in range(3):
        raw[0, 0, 0, TOK : TOK + 32, 128 * i : 128 * (i + 1)] = pair[32 * i : 32 * (i + 1)]
    load_cot.wait()
    gat[0, 0, 1] = (jnp.dot(sel_b, cot[...], preferred_element_type=F32) * scale).astype(BF)

    load_raw.wait()
    pl.semaphore_wait(barrier, 4 + NE - 1)

    started = []
    count = [0]

    def remote(src, dst, device):
        i = count[0]
        count[0] += 1
        copy = pltpu.make_async_remote_copy(
            src_ref=src, dst_ref=dst, send_sem=ssem.at[i], recv_sem=rsem.at[i],
            device_id=device, device_id_type=MESH,
        )
        return copy

    def go(copy):
        copy.start()
        started.append(copy)

    class Gather:
        def __init__(self, axis, at):
            self.plus, self.minus = peer(axis, 1), peer(axis, -1)
            self.at = at
            self.p, self.m, self.f = {}, {}, {}
            for arr in (0, 1):
                self.p[arr] = remote(at(0, arr), at(3, arr), self.plus)
                self.m[arr] = remote(at(0, arr), at(1, arr), self.minus)
            self.f[0] = remote(at(3, 0), at(2, 0), self.plus)
            self.f[1] = remote(at(1, 1), at(2, 1), self.minus)

        def start(self, arr):
            first, second = (self.p, self.m) if arr == 0 else (self.m, self.p)
            go(first[arr])
            go(second[arr])

        def fwd(self, arr):
            (self.p if arr == 0 else self.m)[arr].wait_recv()
            go(self.f[arr])

        def near(self, arr):
            (self.m if arr == 0 else self.p)[arr].wait_recv()

        def far(self, arr):
            self.f[arr].wait_recv()

    CHUNKS = tuple(zip(EDGES[:-1], EDGES[1:]))
    def cut(i):
        return pl.ds(i * (D // 2), D // 2)

    def piece(i):
        return pl.ds(i * 80, 80)

    a1 = Gather("z", lambda i, part: gat.at[i, 0, 1, :, cut(part)])
    a2 = [
        Gather("x", functools.partial(lambda u, i, part: gat.at[u, i, 1, :, cut(part)], u))
        for u in range(4)
    ]
    def sides(g):
        return slice(1, 3) if g == "s" else (0 if g == 0 else 3)

    c1 = Gather("z", lambda i, part: raw.at[0, POS[i], 0, piece(part)])
    c2 = {
        g: Gather("x", functools.partial(lambda g, i, part: raw.at[0, sides(g), POS[i], piece(part)], g))
        for g in (0, "s", 2)
    }
    cy = {
        (u, v): Gather(
            "y",
            functools.partial(
                lambda u, v, i, part: raw.at[i, sides(u), sides(v), pl.ds(64 * part, 64)], u, v
            ),
        )
        for u in (0, "s", 2)
        for v in (0, "s", 2)
        if (u, v) != (0, 0)
    }

    def sibling(u, v):
        return pltpu.make_async_remote_copy(
            src_ref=twin.at[u, v], dst_ref=gat.at[u, v, 0, :, pl.ds(half, D // 2)],
            send_sem=ts.at[4 * u + v], recv_sem=tr.at[4 * u + v],
            device_id=(dp, slot * 2 + 1 - core), device_id_type=MESH,
        )

    def from_sibling(u, v):
        other = pl.multiple_of((1 - core) * (D // 2), 128)
        return pltpu.make_async_remote_copy(
            src_ref=twin.at[u, v], dst_ref=gat.at[u, v, 0, :, pl.ds(other, D // 2)],
            send_sem=ts.at[4 * u + v], recv_sem=tr.at[4 * u + v],
            device_id=(dp, slot * 2 + 1 - core), device_id_type=MESH,
        )

    def pick(u, v):
        both = jnp.concatenate(
            [raw[0, POS[u], POS[v], TOK : TOK + 32, 128 * i : 128 * (i + 1)] for i in range(3)], axis=0
        )
        for r in range(4):
            res = jnp.dot(both, raw[r, POS[u], POS[v], :TOK], preferred_element_type=F32).astype(BF)
            c = ((y + r) % 4) * 384
            gat[u, v, 0, :, pl.ds(pl.multiple_of(half + c, 128), 384)] = res[:CAP]
            twin[u, v, :, pl.ds(pl.multiple_of(c, 128), 384)] = res[CAP:]
        sibling(u, v).start()

    def token_rows(u):
        for v in range(4):
            if (u, v) != (0, 0):
                from_sibling(u, v).wait_recv()

    def finish(ring):
        ring.near(0)
        ring.near(1)
        ring.far(0)
        ring.far(1)

    def rows(ref):
        return ref.reshape(4 * CAP, ref.shape[-1])

    def batch(u):
        t = rows(gat[u, :, 0])
        pre = jnp.dot(t, gate[...], preferred_element_type=F32)
        back = lax.dot_general(
            rows(gat[u, :, 1]), down[...], (((1,), (1,)), ((), ())), preferred_element_type=F32
        )
        s = jax.nn.sigmoid(pre)
        act = (pre * s).astype(BF)
        gp = (back * s * (1.0 + pre * (1.0 - s))).astype(BF)
        act_s[u] = act
        gp_s[u] = gp

        def cols(j, carry):
            c = pl.ds(pl.multiple_of(j * 512, 512), 512)
            o = jnp.dot(act_s[u], down[:, c], preferred_element_type=F32).astype(BF)
            par[u, :, 0, :, c] = o.reshape(4, CAP, 512)
            b = lax.dot_general(
                gp_s[u], gate[c, :], (((1,), (1,)), ((), ())), preferred_element_type=F32
            ).astype(BF)
            par[u, :, 1, :, c] = b.reshape(4, CAP, 512)
            return carry

        lax.fori_loop(0, D // 512, cols, 0)

    def drain():
        for copy in started:
            copy.wait_send()
    class Reduce:
        def __init__(self, axis, at, land, c):
            plus, minus = peer(axis, 1), peer(axis, -1)
            self.at, self.land, self.c = at, land, c
            self.f0 = remote(at(2, 0), land(0, 0), plus)
            self.f1 = remote(at(2, 1), land(0, 1), minus)
            self.l1 = remote(at(1, 1), land(1, 1), plus)
            self.r0 = remote(at(3, 0), land(2, 0), minus)
            self.l0 = remote(at(1, 0), land(1, 0), plus)
            self.r1 = remote(at(3, 1), land(2, 1), minus)

        def start(self):
            go(self.f0)
            go(self.f1)
            go(self.l1)
            go(self.r0)

        def fwd(self):
            for f, copy, i, arr in ((self.f0, self.l0, 1, 0), (self.f1, self.r1, 3, 1)):
                f.wait_recv()
                dst = self.at(i, arr)
                dst[...] = (dst[...].astype(F32) + self.land(0, arr)[...].astype(F32)).astype(BF)
                go(copy)

        def total(self, arr):
            return (
                self.at(0, arr)[...].astype(F32)
                + self.land(1, arr)[...].astype(F32)
                + self.land(2, arr)[...].astype(F32)
            )

        def arrive(self):
            for copy in (self.l1, self.r0, self.l0, self.r1):
                copy.wait_recv()

        def fin(self):
            self.arrive()
            for arr in (0, 1):
                self.at(0, arr)[...] = self.total(arr).astype(BF)

    def stage1(axis, u, c):
        if axis == "x":
            at = lambda i, arr: par.at[u, i, arr, :, c]
        else:
            at = lambda i, arr: par.at[i, u, arr, :, c]
        return Reduce(axis, at, lambda kind, arr: rd1.at[u, kind, arr, :, c], c)

    def stage2(axis, c):
        if axis == "x":
            at = lambda i, arr: par.at[0, i, arr, :, c]
        else:
            at = lambda i, arr: par.at[i, 0, arr, :, c]
        return Reduce(axis, at, lambda kind, arr: rd2.at[kind, arr, :, c], c)

    order = (0, 1, 3, 2)
    every = (slice(None),)
    first = [
        [stage1("x", u, pl.ds(lo, hi - lo)) for u in (every if lo else order)] for lo, hi in CHUNKS
    ]
    second = [stage2("z", pl.ds(lo, hi - lo)) for lo, hi in CHUNKS]
    rb = pl.ds(RA, D - RA)
    first_b = [stage1("z", u, rb) for u in every]
    second_b = stage2("x", rb)

    def home(ring, lo, hi):
        ring.arrive()
        for arr in (0, 1):
            v = ring.total(arr)
            if arr == 0:
                v = v * scale_s[:, :1]
            v = v.astype(BF)
            for i in range((hi - lo) // 128):
                tile = lo // 128 + i
                ex[tile // 8, arr, tile % 8] = v[:, 128 * i : 128 * (i + 1)]

    def exchange(k, e_to, e_from):
        return pltpu.make_async_remote_copy(
            src_ref=ex.at[k, e_to % 2, e_to // 2], dst_ref=rx.at[k, e_from],
            send_sem=xs.at[k, e_to], recv_sem=xr.at[k, e_from],
            device_id=(dp, e_to), device_id_type=MESH,
        )

    def exchange_start(k):
        def one(i, carry):
            exchange(k, (me + i) % NE, me).start()
            return carry

        lax.fori_loop(1, NE, one, 0)
        rx[k, me] = ex[k, core, slot]

    def tile(k, owner):
        return pl.ds(pl.multiple_of(k * 1024 + owner * 128, 128), 128)

    def spread(k, to, frm):
        place = full.at[core, :, tile(k, frm)]
        return pltpu.make_async_remote_copy(
            src_ref=place, dst_ref=place,
            send_sem=os_.at[k, to], recv_sem=or_.at[k, frm],
            device_id=(dp, to * 2 + core), device_id_type=MESH,
        )

    def mix(k):
        def one(i, carry):
            exchange(k, me, (me + i) % NE).wait_recv()
            return carry

        lax.fori_loop(1, NE, one, 0)
        full[core, :, tile(k, slot)] = lax.dot_general(
            sel_s[...], rx[k].reshape(NE * CAP, 128), (((0,), (0,)), ((), ())),
            preferred_element_type=F32,
        ).astype(BF)

        def two(i, carry):
            spread(k, (slot + i) % 8, slot).start()
            return carry

        lax.fori_loop(1, 8, two, 0)

    def relay(k):
        place = full.at[core, :, 1024 * k : 1024 * (k + 1)]
        return pltpu.make_async_remote_copy(
            src_ref=place, dst_ref=place, send_sem=ks.at[k], recv_sem=kr.at[k],
            device_id=(dp, slot * 2 + 1 - core), device_id_type=MESH,
        )

    def keep(k, arr, i):
        part = (arr, slice(None), slice(1024 * k, 1024 * (k + 1)))
        return pltpu.make_async_copy(full.at[part], out.at[part], lsem.at[6 + 2 * k + i])

    def relay_start(k):
        def one(i, carry):
            spread(k, slot, (slot + i) % 8).wait_recv()
            return carry

        lax.fori_loop(1, 8, one, 0)
        relay(k).start()
        keep(k, core, 0).start()

    def relay_finish(k):
        other = full.at[1 - core, :, 1024 * k : 1024 * (k + 1)]
        pltpu.make_async_remote_copy(
            src_ref=other, dst_ref=other, send_sem=ks.at[k], recv_sem=kr.at[k],
            device_id=(dp, slot * 2 + 1 - core), device_id_type=MESH,
        ).wait_recv()
        keep(k, 1 - core, 1).start()

    def grads(j):
        c = pl.ds(512 * j, 512)
        t = gat[:, :, 0, :, c].reshape(NE * CAP, 512)
        g = gat[:, :, 1, :, c].reshape(NE * CAP, 512)
        dg[:, c] = lax.dot_general(
            act_s[...].reshape(NE * CAP, HID), g, (((0,), (0,)), ((), ())),
            preferred_element_type=F32,
        ).astype(BF)
        gg[c, :] = lax.dot_general(
            t, gp_s[...].reshape(NE * CAP, HID), (((0,), (0,)), ((), ())),
            preferred_element_type=F32,
        ).astype(BF)

    def drain():
        for copy in started:
            copy.wait_send()

    def both(f):
        f(0)
        f(1)

    def begin(ring):
        both(ring.start)

    def onward(ring):
        both(ring.fwd)

    both(c1.start)
    begin(c2[0])
    both(a1.start)
    begin(a2[0])
    load_tok.wait()
    gat[0, 0, 0] = jnp.dot(sel_b, tok[...], preferred_element_type=F32).astype(BF)
    onward(c2[0])
    both(c2[0].near)
    begin(cy[0, "s"])
    onward(c1)
    both(c1.near)
    begin(c2["s"])
    begin(cy["s", 0])
    both(c2[0].far)
    begin(cy[0, 2])
    onward(cy[0, "s"])
    onward(a2[0])
    a1.fwd(0)
    a2[3].start(0)
    a1.fwd(1)
    a2[1].start(1)
    both(c1.far)
    begin(c2[2])
    onward(c2["s"])
    onward(cy["s", 0])
    onward(cy[0, 2])
    both(c2["s"].near)
    begin(cy["s", "s"])
    a1.near(0)
    a2[1].start(0)
    a1.near(1)
    a2[3].start(1)
    finish(cy[0, "s"])
    pick(0, 1)
    pick(0, 3)
    onward(c2[2])
    finish(cy[0, 2])
    pick(0, 2)
    a2[3].fwd(0)
    a2[1].fwd(1)
    both(c2["s"].far)
    begin(cy["s", 2])
    a1.far(0)
    a2[2].start(0)
    a1.far(1)
    a2[2].start(1)
    finish(a2[0])
    load_gate.wait()
    load_down.wait()
    token_rows(0)
    batch(0)
    onward(cy["s", "s"])
    begin(cy[2, 0])
    both(c2[2].near)
    begin(cy[2, "s"])
    finish(cy["s", 0])
    pick(1, 0)
    pick(3, 0)
    a2[1].fwd(0)
    a2[3].fwd(1)
    both(c2[2].far)
    begin(cy[2, 2])
    onward(cy["s", 2])
    onward(cy[2, 0])
    finish(cy["s", "s"])
    pick(1, 1)
    pick(1, 3)
    pick(3, 1)
    pick(3, 3)
    onward(cy[2, "s"])
    a2[2].fwd(0)
    a2[2].fwd(1)
    onward(cy[2, 2])
    finish(cy["s", 2])
    pick(1, 2)
    pick(3, 2)
    finish(a2[1])
    token_rows(1)
    batch(1)
    first[0][0].start()
    finish(a2[3])
    token_rows(3)
    batch(3)
    first[0][1].start()
    first[0][2].start()
    finish(cy[2, 0])
    pick(2, 0)
    finish(cy[2, "s"])
    pick(2, 1)
    pick(2, 3)
    finish(cy[2, 2])
    pick(2, 2)
    finish(a2[2])
    token_rows(2)
    batch(2)
    first[0][3].start()
    for ring in first_b:
        ring.start()
    for e in range(NE):
        sel_s[CAP * e : CAP * (e + 1), :] = jnp.where(
            (pos[e : e + 1] == slots) & (member[e : e + 1] > 0.5), 1.0, 0.0
        ).astype(BF)

    n = len(CHUNKS)
    ready = []
    todo = []

    def came(k):
        home(second[k], *CHUNKS[k])
        hi = CHUNKS[k][1]
        if hi in (1024, 2048, RA):
            g = {1024: 0, 2048: 1, RA: 2}[hi]
            if g == 2:
                home(second_b, RA, D)
            exchange_start(g)
            todo.append([g, 0])

    def advance():
        for item in todo:
            g, state = item
            if state < 3:
                (mix, relay_start, relay_finish)[state](g)
                item[1] += 1

    for k in range(n):
        for i, ring in enumerate(first[k]):
            ring.fwd()
            if k == 0:
                grads(i)
            if k + 1 < n and i == 0:
                first[k + 1][0].start()
        if k == 0:
            for ring in first_b:
                ring.fwd()
            grads(4)
            grads(5)
            store_gg = pltpu.make_async_copy(gg, gg_out, lsem.at[2])
            store_dg = pltpu.make_async_copy(dg, dg_out, lsem.at[3])
            store_gg.start()
            store_dg.start()
        if k >= 1:
            second[k - 1].fwd()
        if k >= 2:
            advance()
            came(k - 2)
        for ring in first[k]:
            ring.fin()
        second[k].start()
        if k == 1:
            for ring in first_b:
                ring.fin()
            second_b.start()
        if k == 2:
            second_b.fwd()
    advance()
    came(n - 2)
    second[n - 1].fwd()
    advance()
    came(n - 1)
    advance()
    advance()
    advance()

    store_gg.wait()
    store_dg.wait()
    for k in range(NCH):
        keep(k, core, 0).wait()
        keep(k, 1 - core, 1).wait()
        relay(k).wait_send()

        def last(i, carry, k=k):
            exchange(k, (me + i) % NE, me).wait_send()
            return carry

        lax.fori_loop(1, NE, last, 0)

        def last_spread(i, carry, k=k):
            spread(k, (slot + i) % 8, slot).wait_send()
            return carry

        lax.fori_loop(1, 8, last_spread, 0)
    for u in range(4):
        for v in range(4):
            if (u, v) != (0, 0):
                sibling(u, v).wait_send()
    drain()


N_COPY = 10 * 6 + 5 * 6 * len(EDGES)


def shards(tokens, cotangent, routes, route_weights, gate_weight, down_weight):
    gate_weight = gate_weight.reshape(D, HID)
    down_weight = down_weight.reshape(HID, D)
    out, gg, dg = pl.pallas_call(
        kernel,
        out_shape=(
            jax.ShapeDtypeStruct((2, TOK, D), BF),
            jax.ShapeDtypeStruct((D, HID), BF),
            jax.ShapeDtypeStruct((HID, D), BF),
        ),
        in_specs=[HB, HB, VM, VM, HB, HB],
        out_specs=(HB, HB, HB),
        scratch_shapes=[
            pltpu.VMEM((TOK, D), BF),
            pltpu.VMEM((TOK, D), BF),
            pltpu.VMEM((4, 4, 4, TOK + 32, 384), BF),
            pltpu.VMEM((4, 4, CAP, D // 2), BF),
            pltpu.VMEM((4, 4, 2, CAP, D), BF),
            pltpu.VMEM((4, 4, 2, CAP, D), BF),
            pltpu.VMEM((4, 3, 2, CAP, D), BF),
            pltpu.VMEM((3, 2, CAP, D), BF),
            pltpu.VMEM((D, HID), BF),
            pltpu.VMEM((HID, D), BF),
            pltpu.VMEM((D, HID), BF),
            pltpu.VMEM((HID, D), BF),
            pltpu.VMEM((4, 4 * CAP, HID), BF),
            pltpu.VMEM((4, 4 * CAP, HID), BF),
            pltpu.VMEM((NCH, 2, 8, CAP, 128), BF),
            pltpu.VMEM((NCH, NE, CAP, 128), BF),
            pltpu.VMEM((2, TOK, D), BF),
            pltpu.VMEM((NE * CAP, TOK), BF),
            pltpu.VMEM((CAP, 128), F32),
            pltpu.SemaphoreType.DMA((10 * 6 + 15 * 6 + 5 * 6 * len(EDGES),)),
            pltpu.SemaphoreType.DMA((10 * 6 + 15 * 6 + 5 * 6 * len(EDGES),)),
            pltpu.SemaphoreType.DMA((NCH, NE)),
            pltpu.SemaphoreType.DMA((NCH, NE)),
            pltpu.SemaphoreType.DMA((NCH, 8)),
            pltpu.SemaphoreType.DMA((NCH, 8)),
            pltpu.SemaphoreType.DMA((NCH,)),
            pltpu.SemaphoreType.DMA((NCH,)),
            pltpu.SemaphoreType.DMA((16,)),
            pltpu.SemaphoreType.DMA((16,)),
            pltpu.SemaphoreType.DMA((7 + 2 * NCH,)),
        ],
        compiler_params=pltpu.CompilerParams(
            collective_id=0, has_side_effects=True, vmem_limit_bytes=60 * 2**20
        ),
        cost_estimate=pl.CostEstimate(
            flops=12 * 768 * D * HID, bytes_accessed=2 * 10**7, transcendentals=768 * HID
        ),
        name="moe",
    )(tokens, cotangent, routes.T, route_weights.T, gate_weight, down_weight)
    return out[0], out[1], gg.reshape(1, D, HID), dg.reshape(1, HID, D)


def solution(mesh):
    return jax.shard_map(
        shards,
        mesh=mesh,
        in_specs=(
            P("dp", None),
            P("dp", None),
            P("dp", None),
            P("dp", None),
            P("expert", None, "dp"),
            P("expert", "dp", None),
        ),
        out_specs=(P("dp", None), P("dp", None), P("expert", None, "dp"), P("expert", "dp", None)),
        check_vma=False,
    )
```

```python
import functools

import jax
import jax.numpy as jnp
from jax import lax
from jax.experimental import pallas as pl
from jax.experimental.pallas import tpu as pltpu
from jax.sharding import PartitionSpec as P

MESH = pl.DeviceIdType.MESH
POS = (0, 1, 3, 2)
BF = jnp.bfloat16
F32 = jnp.float32
CAP = 48
TOK = 128
D = 3072
HID = 384
NE = 16
RA = 2688
EDGES = (0, 512, 1024, 1536, 2048, 2432, 2688)
NCH = 3
VM = pl.BlockSpec(memory_space=pltpu.VMEM)
HB = pl.BlockSpec(memory_space=pl.ANY)


def kernel(
    tok_in, cot_in, routes, wts, gate_in, down_in,
    mixed, tgrad, gg_out, dg_out,
    tok, cot, raw, twin, gat, par, rd1, rd2, gate, down, gg, dg, act_s, gp_s, ex, rx, full, sel_s, scale_s,
    ssem, rsem, xs, xr, os_, or_, ks, kr, ts, tr, lsem,
):
    dp = lax.axis_index("dp")
    me = lax.axis_index("expert")
    h, x = dp // 4, dp % 4
    core, slot = me % 2, me // 2
    y, z_lo = me // 4, slot % 2

    def peer(axis, step):
        if axis == "x":
            return (h * 4 + (x + step + 4) % 4, me)
        if axis == "y":
            return (dp, (((y + step + 4) % 4) * 2 + z_lo) * 2 + core)
        return (((h + step + 4) % 4) * 4 + x, me)

    load_tok = pltpu.make_async_copy(tok_in, tok, lsem.at[4])
    load_cot = pltpu.make_async_copy(cot_in, cot, lsem.at[5])
    load_gate = pltpu.make_async_copy(gate_in, gate, lsem.at[0])
    load_down = pltpu.make_async_copy(down_in, down, lsem.at[1])
    half = pl.multiple_of(core * (D // 2), 128)
    load_raw = pltpu.make_async_copy(
        tok_in.at[:, pl.ds(pl.multiple_of(half + y * 384, 128), 384)],
        raw.at[0, 0, 0, pl.ds(0, TOK)],
        lsem.at[6 + 2 * NCH],
    )
    load_raw.start()
    load_tok.start()
    load_cot.start()
    load_gate.start()
    load_down.start()

    barrier = pltpu.get_barrier_semaphore()
    for axis in ("x", "z"):
        for step in (1, -1):
            pl.semaphore_signal(barrier, inc=1, device_id=peer(axis, step), device_id_type=MESH)

    def greet(i, carry):
        pl.semaphore_signal(barrier, inc=1, device_id=(dp, (me + i) % NE), device_id_type=MESH)
        return carry

    lax.fori_loop(1, NE, greet, 0)

    r = routes[...]
    w = wts[...]
    row16 = lax.broadcasted_iota(jnp.int32, (NE, TOK), 0)
    member = jnp.zeros((NE, TOK), F32)
    w_e = jnp.zeros((1, TOK), F32)
    for k in range(4):
        member = member + jnp.where(r[k : k + 1] == row16, 1.0, 0.0)
        w_e = w_e + jnp.where(r[k : k + 1] == me, w[k : k + 1], 0.0)
    before = lax.broadcasted_iota(jnp.int32, (TOK, TOK), 0) < lax.broadcasted_iota(
        jnp.int32, (TOK, TOK), 1
    )
    pos = jnp.dot(
        member.astype(BF), jnp.where(before, 1.0, 0.0).astype(BF), preferred_element_type=F32
    )
    slots = lax.broadcasted_iota(jnp.int32, (CAP, TOK), 0).astype(F32)

    def select(expert):
        mine = jnp.where(row16 == expert, 1.0, 0.0)
        mem_e = jnp.sum(member * mine, axis=0, keepdims=True)
        pos_e = jnp.sum(pos * mine, axis=0, keepdims=True)
        return jnp.where((pos_e == slots) & (mem_e > 0.5), 1.0, 0.0)

    sel = select(me)
    scale = jnp.sum(sel * w_e, axis=1, keepdims=True)
    scale_s[...] = jnp.broadcast_to(scale, (CAP, 128))
    sel_b = sel.astype(BF)
    pair = jnp.concatenate([sel, select(slot * 2 + 1 - core)], axis=0).astype(BF)
    for i in range(3):
        raw[0, 0, 0, TOK : TOK + 32, 128 * i : 128 * (i + 1)] = pair[32 * i : 32 * (i + 1)]
    load_cot.wait()
    gat[0, 0, 1] = (jnp.dot(sel_b, cot[...], preferred_element_type=F32) * scale).astype(BF)

    load_raw.wait()
    pl.semaphore_wait(barrier, 4 + NE - 1)

    started = []
    count = [0]

    def remote(src, dst, device):
        i = count[0]
        count[0] += 1
        copy = pltpu.make_async_remote_copy(
            src_ref=src, dst_ref=dst, send_sem=ssem.at[i], recv_sem=rsem.at[i],
            device_id=device, device_id_type=MESH,
        )
        return copy

    def go(copy):
        copy.start()
        started.append(copy)

    class Gather:
        def __init__(self, axis, at):
            self.plus, self.minus = peer(axis, 1), peer(axis, -1)
            self.at = at
            self.p, self.m, self.f = {}, {}, {}
            for arr in (0, 1):
                self.p[arr] = remote(at(0, arr), at(3, arr), self.plus)
                self.m[arr] = remote(at(0, arr), at(1, arr), self.minus)
            self.f[0] = remote(at(3, 0), at(2, 0), self.plus)
            self.f[1] = remote(at(1, 1), at(2, 1), self.minus)

        def start(self, arr):
            first, second = (self.p, self.m) if arr == 0 else (self.m, self.p)
            go(first[arr])
            go(second[arr])

        def fwd(self, arr):
            (self.p if arr == 0 else self.m)[arr].wait_recv()
            go(self.f[arr])

        def near(self, arr):
            (self.m if arr == 0 else self.p)[arr].wait_recv()

        def far(self, arr):
            self.f[arr].wait_recv()

    CHUNKS = tuple(zip(EDGES[:-1], EDGES[1:]))
    def cut(i):
        return pl.ds(i * (D // 2), D // 2)

    def piece(i):
        return pl.ds(i * 80, 80)

    a1 = Gather("z", lambda i, part: gat.at[i, 0, 1, :, cut(part)])
    a2 = [
        Gather("x", functools.partial(lambda u, i, part: gat.at[u, i, 1, :, cut(part)], u))
        for u in range(4)
    ]
    def sides(g):
        return slice(1, 3) if g == "s" else (0 if g == 0 else 3)

    c1 = Gather("z", lambda i, part: raw.at[0, POS[i], 0, piece(part)])
    c2 = {
        g: Gather("x", functools.partial(lambda g, i, part: raw.at[0, sides(g), POS[i], piece(part)], g))
        for g in (0, "s", 2)
    }
    cy = {
        (u, v): Gather(
            "y",
            functools.partial(
                lambda u, v, i, part: raw.at[i, sides(u), sides(v), pl.ds(64 * part, 64)], u, v
            ),
        )
        for u in (0, "s", 2)
        for v in (0, "s", 2)
        if (u, v) != (0, 0)
    }

    def sibling(u, v):
        return pltpu.make_async_remote_copy(
            src_ref=twin.at[u, v], dst_ref=gat.at[u, v, 0, :, pl.ds(half, D // 2)],
            send_sem=ts.at[4 * u + v], recv_sem=tr.at[4 * u + v],
            device_id=(dp, slot * 2 + 1 - core), device_id_type=MESH,
        )

    def from_sibling(u, v):
        other = pl.multiple_of((1 - core) * (D // 2), 128)
        return pltpu.make_async_remote_copy(
            src_ref=twin.at[u, v], dst_ref=gat.at[u, v, 0, :, pl.ds(other, D // 2)],
            send_sem=ts.at[4 * u + v], recv_sem=tr.at[4 * u + v],
            device_id=(dp, slot * 2 + 1 - core), device_id_type=MESH,
        )

    def pick(u, v):
        both = jnp.concatenate(
            [raw[0, POS[u], POS[v], TOK : TOK + 32, 128 * i : 128 * (i + 1)] for i in range(3)], axis=0
        )
        for r in range(4):
            res = jnp.dot(both, raw[r, POS[u], POS[v], :TOK], preferred_element_type=F32).astype(BF)
            c = ((y + r) % 4) * 384
            gat[u, v, 0, :, pl.ds(pl.multiple_of(half + c, 128), 384)] = res[:CAP]
            twin[u, v, :, pl.ds(pl.multiple_of(c, 128), 384)] = res[CAP:]
        sibling(u, v).start()

    def token_rows(u):
        for v in range(4):
            if (u, v) != (0, 0):
                from_sibling(u, v).wait_recv()

    def finish(ring):
        ring.near(0)
        ring.near(1)
        ring.far(0)
        ring.far(1)

    def rows(ref):
        return ref.reshape(4 * CAP, ref.shape[-1])

    def batch(u):
        t = rows(gat[u, :, 0])
        pre = jnp.dot(t, gate[...], preferred_element_type=F32)
        back = lax.dot_general(
            rows(gat[u, :, 1]), down[...], (((1,), (1,)), ((), ())), preferred_element_type=F32
        )
        s = jax.nn.sigmoid(pre)
        act = (pre * s).astype(BF)
        gp = (back * s * (1.0 + pre * (1.0 - s))).astype(BF)
        act_s[u] = act
        gp_s[u] = gp

        def cols(j, carry):
            c = pl.ds(pl.multiple_of(j * 512, 512), 512)
            o = jnp.dot(act_s[u], down[:, c], preferred_element_type=F32).astype(BF)
            par[u, :, 0, :, c] = o.reshape(4, CAP, 512)
            b = lax.dot_general(
                gp_s[u], gate[c, :], (((1,), (1,)), ((), ())), preferred_element_type=F32
            ).astype(BF)
            par[u, :, 1, :, c] = b.reshape(4, CAP, 512)
            return carry

        lax.fori_loop(0, D // 512, cols, 0)

    def drain(upto):
        for copy in started[:upto]:
            if copy is not None:
                copy.wait_send()
        started[:upto] = [None] * upto
    class Reduce:
        def __init__(self, axis, at, land, c):
            plus, minus = peer(axis, 1), peer(axis, -1)
            self.at, self.land, self.c = at, land, c
            self.f0 = remote(at(2, 0), land(0, 0), plus)
            self.f1 = remote(at(2, 1), land(0, 1), minus)
            self.l1 = remote(at(1, 1), land(1, 1), plus)
            self.r0 = remote(at(3, 0), land(2, 0), minus)
            self.l0 = remote(at(1, 0), land(1, 0), plus)
            self.r1 = remote(at(3, 1), land(2, 1), minus)

        def start(self):
            go(self.f0)
            go(self.f1)
            go(self.l1)
            go(self.r0)

        def fwd(self):
            for f, copy, i, arr in ((self.f0, self.l0, 1, 0), (self.f1, self.r1, 3, 1)):
                f.wait_recv()
                dst = self.at(i, arr)
                dst[...] = (dst[...].astype(F32) + self.land(0, arr)[...].astype(F32)).astype(BF)
                go(copy)

        def total(self, arr):
            return (
                self.at(0, arr)[...].astype(F32)
                + self.land(1, arr)[...].astype(F32)
                + self.land(2, arr)[...].astype(F32)
            )

        def arrive(self):
            for copy in (self.l1, self.r0, self.l0, self.r1):
                copy.wait_recv()

        def fin(self):
            self.arrive()
            for arr in (0, 1):
                self.at(0, arr)[...] = self.total(arr).astype(BF)

    def stage1(axis, u, c):
        if axis == "x":
            at = lambda i, arr: par.at[u, i, arr, :, c]
        else:
            at = lambda i, arr: par.at[i, u, arr, :, c]
        return Reduce(axis, at, lambda kind, arr: rd1.at[u, kind, arr, :, c], c)

    def stage2(axis, c):
        if axis == "x":
            at = lambda i, arr: par.at[0, i, arr, :, c]
        else:
            at = lambda i, arr: par.at[i, 0, arr, :, c]
        return Reduce(axis, at, lambda kind, arr: rd2.at[kind, arr, :, c], c)

    order = (0, 1, 3, 2)
    every = (slice(None),)
    first = [
        [stage1("x", u, pl.ds(lo, hi - lo)) for u in (every if lo else order)] for lo, hi in CHUNKS
    ]
    second = [stage2("z", pl.ds(lo, hi - lo)) for lo, hi in CHUNKS]
    rb = pl.ds(RA, D - RA)
    if RA < D:
        first_b = [stage1("z", u, rb) for u in every]
        second_b = stage2("x", rb)
    else:
        first_b = []

    def home(ring, lo, hi):
        ring.arrive()
        for arr in (0, 1):
            v = ring.total(arr)
            if arr == 0:
                v = v * scale_s[:, :1]
            v = v.astype(BF)
            for i in range((hi - lo) // 128):
                tile = lo // 128 + i
                ex[tile // 8, arr, tile % 8] = v[:, 128 * i : 128 * (i + 1)]

    def exchange(k, e_to, e_from):
        return pltpu.make_async_remote_copy(
            src_ref=ex.at[k, e_to % 2, e_to // 2], dst_ref=rx.at[k, e_from],
            send_sem=xs.at[k, e_to], recv_sem=xr.at[k, e_from],
            device_id=(dp, e_to), device_id_type=MESH,
        )

    def exchange_start(k):
        def one(i, carry):
            exchange(k, (me + i) % NE, me).start()
            return carry

        lax.fori_loop(1, NE, one, 0)
        rx[k, me] = ex[k, core, slot]

    def tile(k, owner):
        return pl.ds(pl.multiple_of(k * 1024 + owner * 128, 128), 128)

    def spread(k, to, frm):
        place = full.at[core, :, tile(k, frm)]
        return pltpu.make_async_remote_copy(
            src_ref=place, dst_ref=place,
            send_sem=os_.at[k, to], recv_sem=or_.at[k, frm],
            device_id=(dp, to * 2 + core), device_id_type=MESH,
        )

    def mix(k):
        def one(i, carry):
            exchange(k, me, (me + i) % NE).wait_recv()
            return carry

        lax.fori_loop(1, NE, one, 0)
        full[core, :, tile(k, slot)] = lax.dot_general(
            sel_s[...], rx[k].reshape(NE * CAP, 128), (((0,), (0,)), ((), ())),
            preferred_element_type=F32,
        ).astype(BF)

        def two(i, carry):
            spread(k, (slot + i) % 8, slot).start()
            return carry

        lax.fori_loop(1, 8, two, 0)

    def relay(k):
        place = full.at[core, :, 1024 * k : 1024 * (k + 1)]
        return pltpu.make_async_remote_copy(
            src_ref=place, dst_ref=place, send_sem=ks.at[k], recv_sem=kr.at[k],
            device_id=(dp, slot * 2 + 1 - core), device_id_type=MESH,
        )

    def keep(k, arr):
        cols = slice(1024 * k, 1024 * (k + 1))
        return pltpu.make_async_copy(
            full.at[arr, :, cols], (mixed, tgrad)[arr].at[:, cols], lsem.at[6 + 2 * k + arr]
        )

    def relay_start(k):
        def one(i, carry):
            spread(k, slot, (slot + i) % 8).wait_recv()
            return carry

        lax.fori_loop(1, 8, one, 0)
        relay(k).start()

    def relay_finish(k):
        other = full.at[1 - core, :, 1024 * k : 1024 * (k + 1)]
        pltpu.make_async_remote_copy(
            src_ref=other, dst_ref=other, send_sem=ks.at[k], recv_sem=kr.at[k],
            device_id=(dp, slot * 2 + 1 - core), device_id_type=MESH,
        ).wait_recv()
        keep(k, 0).start()
        keep(k, 1).start()

    def grads(j):
        c = pl.ds(512 * j, 512)
        t = gat[:, :, 0, :, c].reshape(NE * CAP, 512)
        g = gat[:, :, 1, :, c].reshape(NE * CAP, 512)
        dg[:, c] = lax.dot_general(
            act_s[...].reshape(NE * CAP, HID), g, (((0,), (0,)), ((), ())),
            preferred_element_type=F32,
        ).astype(BF)
        gg[c, :] = lax.dot_general(
            t, gp_s[...].reshape(NE * CAP, HID), (((0,), (0,)), ((), ())),
            preferred_element_type=F32,
        ).astype(BF)

    def drain(upto):
        for copy in started[:upto]:
            if copy is not None:
                copy.wait_send()
        started[:upto] = [None] * upto

    def both(f):
        f(0)
        f(1)

    def begin(ring):
        both(ring.start)

    def onward(ring):
        both(ring.fwd)

    both(c1.start)
    begin(c2[0])
    begin(a2[0])
    load_tok.wait()
    gat[0, 0, 0] = jnp.dot(sel_b, tok[...], preferred_element_type=F32).astype(BF)
    onward(c2[0])
    both(c2[0].near)
    begin(cy[0, "s"])
    onward(c1)
    both(a1.start)
    both(c1.near)
    begin(c2["s"])
    begin(cy["s", 0])
    both(c2[0].far)
    begin(cy[0, 2])
    both(c1.far)
    begin(c2[2])
    onward(cy[0, "s"])
    onward(a2[0])
    onward(c2["s"])
    onward(cy["s", 0])
    onward(cy[0, 2])
    both(c2["s"].near)
    begin(cy["s", "s"])
    a1.fwd(0)
    a2[3].start(0)
    a1.fwd(1)
    a2[1].start(1)
    a1.near(0)
    a2[1].start(0)
    a1.near(1)
    a2[3].start(1)
    finish(cy[0, "s"])
    pick(0, 1)
    pick(0, 3)
    onward(c2[2])
    finish(cy[0, 2])
    pick(0, 2)
    a2[3].fwd(0)
    a2[1].fwd(1)
    both(c2["s"].far)
    begin(cy["s", 2])
    a1.far(0)
    a2[2].start(0)
    a1.far(1)
    a2[2].start(1)
    finish(a2[0])
    load_gate.wait()
    load_down.wait()
    token_rows(0)
    batch(0)
    onward(cy["s", "s"])
    finish(cy["s", 0])
    pick(1, 0)
    pick(3, 0)
    a2[1].fwd(0)
    a2[3].fwd(1)
    onward(cy["s", 2])
    both(c2[2].near)
    begin(cy[2, 0])
    begin(cy[2, "s"])
    finish(cy["s", "s"])
    pick(1, 1)
    pick(1, 3)
    both(c2[2].far)
    begin(cy[2, 2])
    pick(3, 1)
    pick(3, 3)
    a2[2].fwd(0)
    a2[2].fwd(1)
    finish(cy["s", 2])
    pick(1, 2)
    pick(3, 2)
    onward(cy[2, 0])
    onward(cy[2, "s"])
    finish(a2[1])
    token_rows(1)
    batch(1)
    first[0][0].start()
    onward(cy[2, 2])
    finish(cy[2, 0])
    pick(2, 0)
    finish(a2[3])
    token_rows(3)
    batch(3)
    first[0][1].start()
    first[0][2].start()
    finish(cy[2, "s"])
    pick(2, 1)
    pick(2, 3)
    finish(cy[2, 2])
    pick(2, 2)
    finish(a2[2])
    token_rows(2)
    batch(2)
    first[0][3].start()
    for ring in first_b:
        ring.start()
    for e in range(NE):
        sel_s[CAP * e : CAP * (e + 1), :] = jnp.where(
            (pos[e : e + 1] == slots) & (member[e : e + 1] > 0.5), 1.0, 0.0
        ).astype(BF)

    n = len(CHUNKS)
    ready = []
    todo = []

    def came(k):
        home(second[k], *CHUNKS[k])
        hi = CHUNKS[k][1]
        if hi in (1024, 2048, RA):
            g = {1024: 0, 2048: 1, RA: 2}[hi]
            if g == 2:
                if RA < D:
                    home(second_b, RA, D)
            exchange_start(g)
            todo.append([g, 0])

    def advance():
        for item in todo:
            g, state = item
            if state < 3:
                (mix, relay_start, relay_finish)[state](g)
                item[1] += 1

    for k in range(n):
        mark = len(started)
        for i, ring in enumerate(first[k]):
            ring.fwd()
            if k == 0:
                grads(i)
            if k + 1 < n and i == 0:
                first[k + 1][0].start()
        if k == 1:
            for ring in first_b:
                ring.fwd()
        if k == 0:
            grads(4)
            grads(5)
            store_gg = pltpu.make_async_copy(gg, gg_out, lsem.at[2])
            store_dg = pltpu.make_async_copy(dg, dg_out, lsem.at[3])
            store_gg.start()
            store_dg.start()
        if k >= 1:
            second[k - 1].fwd()
        if k >= 2:
            advance()
            came(k - 2)
            drain(old)
        old = mark
        for ring in first[k]:
            ring.fin()
        second[k].start()
        if k == 2 and RA < D:
            for ring in first_b:
                ring.fin()
            second_b.start()
        if k == 3 and RA < D:
            second_b.fwd()
    came(n - 2)
    second[n - 1].fwd()
    came(n - 1)
    mix(1)
    relay_finish(0)
    mix(2)
    relay_start(1)
    drain(old)
    relay_start(2)
    relay_finish(1)
    relay_finish(2)

    store_gg.wait()
    store_dg.wait()
    for k in range(NCH):
        keep(k, 0).wait()
        keep(k, 1).wait()
        relay(k).wait_send()

        def last(i, carry, k=k):
            exchange(k, (me + i) % NE, me).wait_send()
            return carry

        lax.fori_loop(1, NE, last, 0)

        def last_spread(i, carry, k=k):
            spread(k, (slot + i) % 8, slot).wait_send()
            return carry

        lax.fori_loop(1, 8, last_spread, 0)
    for u in range(4):
        for v in range(4):
            if (u, v) != (0, 0):
                sibling(u, v).wait_send()
    drain(len(started))


N_COPY = 10 * 6 + 5 * 6 * len(EDGES)


def shards(tokens, cotangent, routes, route_weights, gate_weight, down_weight):
    gate_weight = gate_weight.reshape(D, HID)
    down_weight = down_weight.reshape(HID, D)
    mixed, tgrad, gg, dg = pl.pallas_call(
        kernel,
        out_shape=(
            jax.ShapeDtypeStruct((TOK, D), BF),
            jax.ShapeDtypeStruct((TOK, D), BF),
            jax.ShapeDtypeStruct((D, HID), BF),
            jax.ShapeDtypeStruct((HID, D), BF),
        ),
        in_specs=[HB, HB, VM, VM, HB, HB],
        out_specs=(HB, HB, HB, HB),
        scratch_shapes=[
            pltpu.VMEM((TOK, D), BF),
            pltpu.VMEM((TOK, D), BF),
            pltpu.VMEM((4, 4, 4, TOK + 32, 384), BF),
            pltpu.VMEM((4, 4, CAP, D // 2), BF),
            pltpu.VMEM((4, 4, 2, CAP, D), BF),
            pltpu.VMEM((4, 4, 2, CAP, D), BF),
            pltpu.VMEM((4, 3, 2, CAP, D), BF),
            pltpu.VMEM((3, 2, CAP, D), BF),
            pltpu.VMEM((D, HID), BF),
            pltpu.VMEM((HID, D), BF),
            pltpu.VMEM((D, HID), BF),
            pltpu.VMEM((HID, D), BF),
            pltpu.VMEM((4, 4 * CAP, HID), BF),
            pltpu.VMEM((4, 4 * CAP, HID), BF),
            pltpu.VMEM((NCH, 2, 8, CAP, 128), BF),
            pltpu.VMEM((NCH, NE, CAP, 128), BF),
            pltpu.VMEM((2, TOK, D), BF),
            pltpu.VMEM((NE * CAP, TOK), BF),
            pltpu.VMEM((CAP, 128), F32),
            pltpu.SemaphoreType.DMA((10 * 6 + 15 * 6 + 5 * 6 * len(EDGES),)),
            pltpu.SemaphoreType.DMA((10 * 6 + 15 * 6 + 5 * 6 * len(EDGES),)),
            pltpu.SemaphoreType.DMA((NCH, NE)),
            pltpu.SemaphoreType.DMA((NCH, NE)),
            pltpu.SemaphoreType.DMA((NCH, 8)),
            pltpu.SemaphoreType.DMA((NCH, 8)),
            pltpu.SemaphoreType.DMA((NCH,)),
            pltpu.SemaphoreType.DMA((NCH,)),
            pltpu.SemaphoreType.DMA((16,)),
            pltpu.SemaphoreType.DMA((16,)),
            pltpu.SemaphoreType.DMA((7 + 2 * NCH,)),
        ],
        compiler_params=pltpu.CompilerParams(
            collective_id=0, has_side_effects=True, vmem_limit_bytes=60 * 2**20
        ),
        cost_estimate=pl.CostEstimate(
            flops=12 * 768 * D * HID, bytes_accessed=2 * 10**7, transcendentals=768 * HID
        ),
        name="moe",
    )(tokens, cotangent, routes.T, route_weights.T, gate_weight, down_weight)
    return mixed, tgrad, gg.reshape(1, D, HID), dg.reshape(1, HID, D)


def solution(mesh):
    return jax.shard_map(
        shards,
        mesh=mesh,
        in_specs=(
            P("dp", None),
            P("dp", None),
            P("dp", None),
            P("dp", None),
            P("expert", None, "dp"),
            P("expert", "dp", None),
        ),
        out_specs=(P("dp", None), P("dp", None), P("expert", None, "dp"), P("expert", "dp", None)),
        check_vma=False,
    )
```

```python
import functools

import jax
import jax.numpy as jnp
from jax import lax
from jax.experimental import pallas as pl
from jax.experimental.pallas import tpu as pltpu
from jax.sharding import PartitionSpec as P

MESH = pl.DeviceIdType.MESH
POS = (0, 1, 3, 2)
BF = jnp.bfloat16
F32 = jnp.float32
CAP = 48
TOK = 128
D = 3072
HID = 384
NE = 16
RA = 2560
GA = 2304
EDGES = (0, 512, 1024, 1536, 2048, 2304, 2560)
NCH = 3
VM = pl.BlockSpec(memory_space=pltpu.VMEM)
HB = pl.BlockSpec(memory_space=pl.ANY)


def kernel(
    tok_in, cot_in, routes, wts, gate_in, down_in,
    mixed, tgrad, gg, dg,
    tok, cot, raw, twin, gat, par, rd1, rd2, gate, down, act_s, gp_s, ex, rx, full, sel_s, scale_s,
    ssem, rsem, xs, xr, os_, or_, ks, kr, ts, tr, lsem,
):
    dp = lax.axis_index("dp")
    me = lax.axis_index("expert")
    h, x = dp // 4, dp % 4
    core, slot = me % 2, me // 2
    y, z_lo = me // 4, slot % 2

    def peer(axis, step):
        if axis == "x":
            return (h * 4 + (x + step + 4) % 4, me)
        if axis == "y":
            return (dp, (((y + step + 4) % 4) * 2 + z_lo) * 2 + core)
        return (((h + step + 4) % 4) * 4 + x, me)

    load_tok = pltpu.make_async_copy(tok_in, tok, lsem.at[4])
    load_cot = pltpu.make_async_copy(cot_in, cot, lsem.at[5])
    load_gate = pltpu.make_async_copy(gate_in, gate, lsem.at[0])
    load_down = pltpu.make_async_copy(down_in, down, lsem.at[1])
    half = pl.multiple_of(core * (D // 2), 128)
    load_raw = pltpu.make_async_copy(
        tok_in.at[:, pl.ds(pl.multiple_of(half + y * 384, 128), 384)],
        raw.at[0, 0, 0, pl.ds(0, TOK)],
        lsem.at[6 + 2 * NCH],
    )
    load_raw.start()
    load_tok.start()
    load_cot.start()
    load_gate.start()
    load_down.start()

    barrier = pltpu.get_barrier_semaphore()
    for axis in ("x", "z"):
        for step in (1, -1):
            pl.semaphore_signal(barrier, inc=1, device_id=peer(axis, step), device_id_type=MESH)

    def greet(i, carry):
        pl.semaphore_signal(barrier, inc=1, device_id=(dp, (me + i) % NE), device_id_type=MESH)
        return carry

    lax.fori_loop(1, NE, greet, 0)

    r = routes[...]
    w = wts[...]
    row16 = lax.broadcasted_iota(jnp.int32, (NE, TOK), 0)
    member = jnp.zeros((NE, TOK), F32)
    w_e = jnp.zeros((1, TOK), F32)
    for k in range(4):
        member = member + jnp.where(r[k : k + 1] == row16, 1.0, 0.0)
        w_e = w_e + jnp.where(r[k : k + 1] == me, w[k : k + 1], 0.0)
    before = lax.broadcasted_iota(jnp.int32, (TOK, TOK), 0) < lax.broadcasted_iota(
        jnp.int32, (TOK, TOK), 1
    )
    pos = jnp.dot(
        member.astype(BF), jnp.where(before, 1.0, 0.0).astype(BF), preferred_element_type=F32
    )
    slots = lax.broadcasted_iota(jnp.int32, (CAP, TOK), 0).astype(F32)

    def select(expert):
        mine = jnp.where(row16 == expert, 1.0, 0.0)
        mem_e = jnp.sum(member * mine, axis=0, keepdims=True)
        pos_e = jnp.sum(pos * mine, axis=0, keepdims=True)
        return jnp.where((pos_e == slots) & (mem_e > 0.5), 1.0, 0.0)

    sel = select(me)
    scale = jnp.sum(sel * w_e, axis=1, keepdims=True)
    scale_s[...] = jnp.broadcast_to(scale, (CAP, 128))
    sel_b = sel.astype(BF)
    pair = jnp.concatenate([sel, select(slot * 2 + 1 - core)], axis=0).astype(BF)
    for i in range(3):
        raw[0, 0, 0, TOK : TOK + 32, 128 * i : 128 * (i + 1)] = pair[32 * i : 32 * (i + 1)]
    load_raw.wait()
    pl.semaphore_wait(barrier, 4 + NE - 1)

    started = []
    count = [0]

    def remote(src, dst, device):
        i = count[0]
        count[0] += 1
        copy = pltpu.make_async_remote_copy(
            src_ref=src, dst_ref=dst, send_sem=ssem.at[i], recv_sem=rsem.at[i],
            device_id=device, device_id_type=MESH,
        )
        return copy

    def go(copy):
        copy.start()
        started.append(copy)

    class Gather:
        def __init__(self, axis, at):
            self.plus, self.minus = peer(axis, 1), peer(axis, -1)
            self.at = at
            self.p, self.m, self.f = {}, {}, {}
            for arr in (0, 1):
                self.p[arr] = remote(at(0, arr), at(3, arr), self.plus)
                self.m[arr] = remote(at(0, arr), at(1, arr), self.minus)
            self.f[0] = remote(at(3, 0), at(2, 0), self.plus)
            self.f[1] = remote(at(1, 1), at(2, 1), self.minus)

        def start(self, arr):
            first, second = (self.p, self.m) if arr == 0 else (self.m, self.p)
            go(first[arr])
            go(second[arr])

        def fwd(self, arr):
            (self.p if arr == 0 else self.m)[arr].wait_recv()
            go(self.f[arr])

        def near(self, arr):
            (self.m if arr == 0 else self.p)[arr].wait_recv()

        def far(self, arr):
            self.f[arr].wait_recv()

    CHUNKS = tuple(zip(EDGES[:-1], EDGES[1:]))
    def cut(i):
        return pl.ds(i * (GA // 2), GA // 2)

    def rest(i):
        return pl.ds(GA + i * ((D - GA) // 2), (D - GA) // 2)

    def piece(i):
        return pl.ds(i * 80, 80)

    a1 = Gather("z", lambda i, part: gat.at[i, 0, 1, :, cut(part)])
    a2 = [
        Gather("x", functools.partial(lambda u, i, part: gat.at[u, i, 1, :, cut(part)], u))
        for u in range(4)
    ]
    def sides(g):
        return slice(1, 3) if g == "s" else (0 if g == 0 else 3)

    b1 = Gather("x", lambda i, part: gat.at[0, i, 1, :, rest(part)])
    b2 = [
        Gather("z", functools.partial(lambda u, i, part: gat.at[i, u, 1, :, rest(part)], u))
        for u in range(4)
    ]
    c1 = Gather("z", lambda i, part: raw.at[0, POS[i], 0, piece(part)])
    c2 = {
        g: Gather("x", functools.partial(lambda g, i, part: raw.at[0, sides(g), POS[i], piece(part)], g))
        for g in (0, "s", 2)
    }
    cy = {
        (u, v): Gather(
            "y",
            functools.partial(
                lambda u, v, i, part: raw.at[i, sides(u), sides(v), pl.ds(64 * part, 64)], u, v
            ),
        )
        for u in (0, "s", 2)
        for v in (0, "s", 2)
        if (u, v) != (0, 0)
    }

    def sibling(u, v):
        return pltpu.make_async_remote_copy(
            src_ref=twin.at[u, v], dst_ref=gat.at[u, v, 0, :, pl.ds(half, D // 2)],
            send_sem=ts.at[4 * u + v], recv_sem=tr.at[4 * u + v],
            device_id=(dp, slot * 2 + 1 - core), device_id_type=MESH,
        )

    def from_sibling(u, v):
        other = pl.multiple_of((1 - core) * (D // 2), 128)
        return pltpu.make_async_remote_copy(
            src_ref=twin.at[u, v], dst_ref=gat.at[u, v, 0, :, pl.ds(other, D // 2)],
            send_sem=ts.at[4 * u + v], recv_sem=tr.at[4 * u + v],
            device_id=(dp, slot * 2 + 1 - core), device_id_type=MESH,
        )

    def pick(u, v):
        both = jnp.concatenate(
            [raw[0, POS[u], POS[v], TOK : TOK + 32, 128 * i : 128 * (i + 1)] for i in range(3)], axis=0
        )
        for r in range(4):
            res = jnp.dot(both, raw[r, POS[u], POS[v], :TOK], preferred_element_type=F32).astype(BF)
            c = ((y + r) % 4) * 384
            gat[u, v, 0, :, pl.ds(pl.multiple_of(half + c, 128), 384)] = res[:CAP]
            twin[u, v, :, pl.ds(pl.multiple_of(c, 128), 384)] = res[CAP:]
        sibling(u, v).start()

    def token_rows(u):
        for v in range(4):
            if (u, v) != (0, 0):
                from_sibling(u, v).wait_recv()

    def finish(ring):
        ring.near(0)
        ring.near(1)
        ring.far(0)
        ring.far(1)

    def rows(ref):
        return ref.reshape(4 * CAP, ref.shape[-1])

    def batch(u):
        t = rows(gat[u, :, 0])
        pre = jnp.dot(t, gate[...], preferred_element_type=F32)
        back = lax.dot_general(
            rows(gat[u, :, 1]), down[...], (((1,), (1,)), ((), ())), preferred_element_type=F32
        )
        s = jax.nn.sigmoid(pre)
        act = (pre * s).astype(BF)
        gp = (back * s * (1.0 + pre * (1.0 - s))).astype(BF)
        act_s[u] = act
        gp_s[u] = gp

        def cols(j, carry):
            c = pl.ds(pl.multiple_of(j * 512, 512), 512)
            o = jnp.dot(act_s[u], down[:, c], preferred_element_type=F32).astype(BF)
            par[u, :, 0, :, c] = o.reshape(4, CAP, 512)
            b = lax.dot_general(
                gp_s[u], gate[c, :], (((1,), (1,)), ((), ())), preferred_element_type=F32
            ).astype(BF)
            par[u, :, 1, :, c] = b.reshape(4, CAP, 512)
            return carry

        lax.fori_loop(0, D // 512, cols, 0)

    def drain(upto):
        for copy in started[:upto]:
            if copy is not None:
                copy.wait_send()
        started[:upto] = [None] * upto
    class Reduce:
        def __init__(self, axis, at, land, c):
            plus, minus = peer(axis, 1), peer(axis, -1)
            self.at, self.land, self.c = at, land, c
            self.f0 = remote(at(2, 0), land(0, 0), plus)
            self.f1 = remote(at(2, 1), land(0, 1), minus)
            self.l1 = remote(at(1, 1), land(1, 1), plus)
            self.r0 = remote(at(3, 0), land(2, 0), minus)
            self.l0 = remote(at(1, 0), land(1, 0), plus)
            self.r1 = remote(at(3, 1), land(2, 1), minus)

        def start(self):
            go(self.f0)
            go(self.f1)
            go(self.l1)
            go(self.r0)

        def fwd(self):
            for f, copy, i, arr in ((self.f0, self.l0, 1, 0), (self.f1, self.r1, 3, 1)):
                f.wait_recv()
                dst = self.at(i, arr)
                dst[...] = (dst[...].astype(F32) + self.land(0, arr)[...].astype(F32)).astype(BF)
                go(copy)

        def total(self, arr):
            return (
                self.at(0, arr)[...].astype(F32)
                + self.land(1, arr)[...].astype(F32)
                + self.land(2, arr)[...].astype(F32)
            )

        def arrive(self):
            for copy in (self.l1, self.r0, self.l0, self.r1):
                copy.wait_recv()

        def fin(self):
            self.arrive()
            for arr in (0, 1):
                self.at(0, arr)[...] = self.total(arr).astype(BF)

    def stage1(axis, u, c):
        if axis == "x":
            at = lambda i, arr: par.at[u, i, arr, :, c]
        else:
            at = lambda i, arr: par.at[i, u, arr, :, c]
        return Reduce(axis, at, lambda kind, arr: rd1.at[u, kind, arr, :, c], c)

    def stage2(axis, c):
        if axis == "x":
            at = lambda i, arr: par.at[0, i, arr, :, c]
        else:
            at = lambda i, arr: par.at[i, 0, arr, :, c]
        return Reduce(axis, at, lambda kind, arr: rd2.at[kind, arr, :, c], c)

    order = (0, 1, 3, 2)
    every = (slice(None),)
    first = [
        [stage1("x", u, pl.ds(lo, hi - lo)) for u in (every if lo else order)] for lo, hi in CHUNKS
    ]
    second = [stage2("z", pl.ds(lo, hi - lo)) for lo, hi in CHUNKS]
    rb = pl.ds(RA, D - RA)
    if RA < D:
        first_b = [stage1("z", u, rb) for u in every]
        second_b = stage2("x", rb)
    else:
        first_b = []

    def home(ring, lo, hi):
        ring.arrive()
        for arr in (0, 1):
            v = ring.total(arr)
            if arr == 0:
                v = v * scale_s[:, :1]
            v = v.astype(BF)
            for i in range((hi - lo) // 128):
                tile = lo // 128 + i
                ex[tile // 8, arr, tile % 8] = v[:, 128 * i : 128 * (i + 1)]

    def exchange(k, e_to, e_from):
        return pltpu.make_async_remote_copy(
            src_ref=ex.at[k, e_to % 2, e_to // 2], dst_ref=rx.at[k, e_from],
            send_sem=xs.at[k, e_to], recv_sem=xr.at[k, e_from],
            device_id=(dp, e_to), device_id_type=MESH,
        )

    def exchange_start(k):
        def one(i, carry):
            exchange(k, (me + i) % NE, me).start()
            return carry

        lax.fori_loop(1, NE, one, 0)
        rx[k, me] = ex[k, core, slot]

    def tile(k, owner):
        return pl.ds(pl.multiple_of(k * 1024 + owner * 128, 128), 128)

    def spread(k, to, frm):
        place = full.at[core, :, tile(k, frm)]
        return pltpu.make_async_remote_copy(
            src_ref=place, dst_ref=place,
            send_sem=os_.at[k, to], recv_sem=or_.at[k, frm],
            device_id=(dp, to * 2 + core), device_id_type=MESH,
        )

    def mix(k):
        def one(i, carry):
            exchange(k, me, (me + i) % NE).wait_recv()
            return carry

        lax.fori_loop(1, NE, one, 0)
        full[core, :, tile(k, slot)] = lax.dot_general(
            sel_s[...], rx[k].reshape(NE * CAP, 128), (((0,), (0,)), ((), ())),
            preferred_element_type=F32,
        ).astype(BF)

        def two(i, carry):
            spread(k, (slot + i) % 8, slot).start()
            return carry

        lax.fori_loop(1, 8, two, 0)

    def relay(k):
        place = full.at[core, :, 1024 * k : 1024 * (k + 1)]
        return pltpu.make_async_remote_copy(
            src_ref=place, dst_ref=place, send_sem=ks.at[k], recv_sem=kr.at[k],
            device_id=(dp, slot * 2 + 1 - core), device_id_type=MESH,
        )

    def keep(k, arr):
        cols = slice(1024 * k, 1024 * (k + 1))
        return pltpu.make_async_copy(
            full.at[arr, :, cols], (mixed, tgrad)[arr].at[:, cols], lsem.at[6 + 2 * k + arr]
        )

    def relay_start(k):
        def one(i, carry):
            spread(k, slot, (slot + i) % 8).wait_recv()
            return carry

        lax.fori_loop(1, 8, one, 0)
        relay(k).start()

    def relay_finish(k):
        other = full.at[1 - core, :, 1024 * k : 1024 * (k + 1)]
        pltpu.make_async_remote_copy(
            src_ref=other, dst_ref=other, send_sem=ks.at[k], recv_sem=kr.at[k],
            device_id=(dp, slot * 2 + 1 - core), device_id_type=MESH,
        ).wait_recv()
        keep(k, 0).start()
        keep(k, 1).start()

    def grads(j):
        c = pl.ds(512 * j, 512)
        t = gat[:, :, 0, :, c].reshape(NE * CAP, 512)
        g = gat[:, :, 1, :, c].reshape(NE * CAP, 512)
        dg[:, c] = lax.dot_general(
            act_s[...].reshape(NE * CAP, HID), g, (((0,), (0,)), ((), ())),
            preferred_element_type=F32,
        ).astype(BF)
        gg[c, :] = lax.dot_general(
            t, gp_s[...].reshape(NE * CAP, HID), (((0,), (0,)), ((), ())),
            preferred_element_type=F32,
        ).astype(BF)

    def drain(upto):
        for copy in started[:upto]:
            if copy is not None:
                copy.wait_send()
        started[:upto] = [None] * upto

    def both(f):
        f(0)
        f(1)

    def begin(ring):
        both(ring.start)

    def onward(ring):
        both(ring.fwd)

    both(c1.start)
    begin(c2[0])
    load_cot.wait()
    gat[0, 0, 1] = (jnp.dot(sel_b, cot[...], preferred_element_type=F32) * scale).astype(BF)
    begin(b1)
    begin(a2[0])
    load_tok.wait()
    gat[0, 0, 0] = jnp.dot(sel_b, tok[...], preferred_element_type=F32).astype(BF)
    onward(c2[0])
    both(c2[0].near)
    begin(cy[0, "s"])
    onward(c1)
    both(a1.start)
    both(c1.near)
    begin(c2["s"])
    begin(cy["s", 0])
    both(c2[0].far)
    begin(cy[0, 2])
    both(c1.far)
    begin(c2[2])
    onward(cy[0, "s"])
    onward(b1)
    begin(b2[0])
    onward(a2[0])
    onward(c2["s"])
    onward(cy["s", 0])
    onward(cy[0, 2])
    both(c2["s"].near)
    begin(cy["s", "s"])
    a1.fwd(0)
    a2[3].start(0)
    a1.fwd(1)
    a2[1].start(1)
    a1.near(0)
    a2[1].start(0)
    a1.near(1)
    a2[3].start(1)
    finish(cy[0, "s"])
    pick(0, 1)
    pick(0, 3)
    onward(c2[2])
    finish(cy[0, 2])
    pick(0, 2)
    a2[3].fwd(0)
    a2[1].fwd(1)
    both(c2["s"].far)
    begin(cy["s", 2])
    a1.far(0)
    a2[2].start(0)
    a1.far(1)
    a2[2].start(1)
    both(b1.near)
    begin(b2[1])
    begin(b2[3])
    onward(b2[0])
    both(b1.far)
    begin(b2[2])
    finish(a2[0])
    load_gate.wait()
    load_down.wait()
    token_rows(0)
    batch(0)
    onward(cy["s", "s"])
    finish(cy["s", 0])
    pick(1, 0)
    pick(3, 0)
    a2[1].fwd(0)
    a2[3].fwd(1)
    onward(cy["s", 2])
    onward(b2[1])
    onward(b2[3])
    both(c2[2].near)
    begin(cy[2, 0])
    begin(cy[2, "s"])
    finish(cy["s", "s"])
    pick(1, 1)
    pick(1, 3)
    both(c2[2].far)
    begin(cy[2, 2])
    pick(3, 1)
    pick(3, 3)
    onward(b2[2])
    a2[2].fwd(0)
    a2[2].fwd(1)
    finish(cy["s", 2])
    pick(1, 2)
    pick(3, 2)
    onward(cy[2, 0])
    onward(cy[2, "s"])
    for ring in b2:
        both(ring.near)
    finish(a2[1])
    token_rows(1)
    batch(1)
    first[0][0].start()
    onward(cy[2, 2])
    finish(cy[2, 0])
    pick(2, 0)
    finish(a2[3])
    token_rows(3)
    batch(3)
    first[0][1].start()
    first[0][2].start()
    finish(cy[2, "s"])
    pick(2, 1)
    pick(2, 3)
    finish(cy[2, 2])
    pick(2, 2)
    for ring in b2:
        both(ring.far)
    finish(a2[2])
    token_rows(2)
    batch(2)
    first[0][3].start()
    for ring in first_b:
        ring.start()
    for e in range(NE):
        sel_s[CAP * e : CAP * (e + 1), :] = jnp.where(
            (pos[e : e + 1] == slots) & (member[e : e + 1] > 0.5), 1.0, 0.0
        ).astype(BF)

    n = len(CHUNKS)
    ready = []
    todo = []

    def came(k):
        home(second[k], *CHUNKS[k])
        hi = CHUNKS[k][1]
        if hi in (1024, 2048, RA):
            g = {1024: 0, 2048: 1, RA: 2}[hi]
            if g == 2:
                if RA < D:
                    home(second_b, RA, D)
            exchange_start(g)
            todo.append([g, 0])

    def advance():
        for item in todo:
            g, state = item
            if state < 3:
                (mix, relay_start, relay_finish)[state](g)
                item[1] += 1

    for k in range(n):
        mark = len(started)
        for i, ring in enumerate(first[k]):
            ring.fwd()
            if k == 0:
                grads(i)
            if k + 1 < n and i == 0:
                first[k + 1][0].start()
        if k == 1:
            for ring in first_b:
                ring.fwd()
        if k == 0:
            grads(4)
            grads(5)
        if k >= 1:
            second[k - 1].fwd()
        if k >= 2:
            advance()
            came(k - 2)
            drain(old)
        old = mark
        for ring in first[k]:
            ring.fin()
        second[k].start()
        if k == 2 and RA < D:
            for ring in first_b:
                ring.fin()
            second_b.start()
        if k == 3 and RA < D:
            second_b.fwd()
    came(n - 2)
    second[n - 1].fwd()
    came(n - 1)
    mix(1)
    relay_finish(0)
    mix(2)
    relay_start(1)
    drain(old)
    relay_start(2)
    relay_finish(1)
    relay_finish(2)

    for k in range(NCH):
        keep(k, 0).wait()
        keep(k, 1).wait()
        relay(k).wait_send()

        def last(i, carry, k=k):
            exchange(k, (me + i) % NE, me).wait_send()
            return carry

        lax.fori_loop(1, NE, last, 0)

        def last_spread(i, carry, k=k):
            spread(k, (slot + i) % 8, slot).wait_send()
            return carry

        lax.fori_loop(1, 8, last_spread, 0)
    for u in range(4):
        for v in range(4):
            if (u, v) != (0, 0):
                sibling(u, v).wait_send()
    drain(len(started))


N_COPY = 10 * 6 + 5 * 6 * len(EDGES)


def shards(tokens, cotangent, routes, route_weights, gate_weight, down_weight):
    gate_weight = gate_weight.reshape(D, HID)
    down_weight = down_weight.reshape(HID, D)
    mixed, tgrad, gg, dg = pl.pallas_call(
        kernel,
        out_shape=(
            pltpu.VMEM((TOK, D), BF),
            pltpu.VMEM((TOK, D), BF),
            pltpu.VMEM((D, HID), BF),
            pltpu.VMEM((HID, D), BF),
        ),
        in_specs=[HB, HB, VM, VM, HB, HB],
        out_specs=(VM, VM, VM, VM),
        scratch_shapes=[
            pltpu.VMEM((TOK, D), BF),
            pltpu.VMEM((TOK, D), BF),
            pltpu.VMEM((4, 4, 4, TOK + 32, 384), BF),
            pltpu.VMEM((4, 4, CAP, D // 2), BF),
            pltpu.VMEM((4, 4, 2, CAP, D), BF),
            pltpu.VMEM((4, 4, 2, CAP, D), BF),
            pltpu.VMEM((4, 3, 2, CAP, D), BF),
            pltpu.VMEM((3, 2, CAP, D), BF),
            pltpu.VMEM((D, HID), BF),
            pltpu.VMEM((HID, D), BF),
            pltpu.VMEM((4, 4 * CAP, HID), BF),
            pltpu.VMEM((4, 4 * CAP, HID), BF),
            pltpu.VMEM((NCH, 2, 8, CAP, 128), BF),
            pltpu.VMEM((NCH, NE, CAP, 128), BF),
            pltpu.VMEM((2, TOK, D), BF),
            pltpu.VMEM((NE * CAP, TOK), BF),
            pltpu.VMEM((CAP, 128), F32),
            pltpu.SemaphoreType.DMA((15 * 6 + 15 * 6 + 5 * 6 * len(EDGES),)),
            pltpu.SemaphoreType.DMA((15 * 6 + 15 * 6 + 5 * 6 * len(EDGES),)),
            pltpu.SemaphoreType.DMA((NCH, NE)),
            pltpu.SemaphoreType.DMA((NCH, NE)),
            pltpu.SemaphoreType.DMA((NCH, 8)),
            pltpu.SemaphoreType.DMA((NCH, 8)),
            pltpu.SemaphoreType.DMA((NCH,)),
            pltpu.SemaphoreType.DMA((NCH,)),
            pltpu.SemaphoreType.DMA((16,)),
            pltpu.SemaphoreType.DMA((16,)),
            pltpu.SemaphoreType.DMA((7 + 2 * NCH,)),
        ],
        compiler_params=pltpu.CompilerParams(
            collective_id=0, has_side_effects=True, vmem_limit_bytes=56 * 2**20
        ),
        cost_estimate=pl.CostEstimate(
            flops=12 * 768 * D * HID, bytes_accessed=2 * 10**7, transcendentals=768 * HID
        ),
        name="moe",
    )(tokens, cotangent, routes.T, route_weights.T, gate_weight, down_weight)
    return mixed, tgrad, gg.reshape(1, D, HID), dg.reshape(1, HID, D)


def solution(mesh):
    return jax.shard_map(
        shards,
        mesh=mesh,
        in_specs=(
            P("dp", None),
            P("dp", None),
            P("dp", None),
            P("dp", None),
            P("expert", None, "dp"),
            P("expert", "dp", None),
        ),
        out_specs=(P("dp", None), P("dp", None), P("expert", None, "dp"), P("expert", "dp", None)),
        check_vma=False,
    )
```

```python
import functools

import jax
import jax.numpy as jnp
from jax import lax
from jax.experimental import pallas as pl
from jax.experimental.pallas import tpu as pltpu
from jax.sharding import PartitionSpec as P

MESH = pl.DeviceIdType.MESH
POS = (0, 1, 3, 2)
BF = jnp.bfloat16
F32 = jnp.float32
CAP = 48
TOK = 128
D = 3072
HID = 384
NE = 16
RA = 2560
GA = 2304
EDGES = (0, 512, 1024, 1536, 2048, 2304, 2560)
NCH = 3
VM = pl.BlockSpec(memory_space=pltpu.VMEM)
HB = pl.BlockSpec(memory_space=pl.ANY)


def kernel(
    tok_in, cot_in, routes, wts, gate_in, down_in,
    mixed, tgrad, gg, dg,
    tok, cot, raw, twin, gat, par, rd1, rd2, gate, down, act_s, gp_s, ex, rx, full, sel_s, scale_s,
    ssem, rsem, xs, xr, os_, or_, ks, kr, ts, tr, lsem,
):
    dp = lax.axis_index("dp")
    me = lax.axis_index("expert")
    h, x = dp // 4, dp % 4
    core, slot = me % 2, me // 2
    y, z_lo = me // 4, slot % 2

    def peer(axis, step):
        if axis == "x":
            return (h * 4 + (x + step + 4) % 4, me)
        if axis == "y":
            return (dp, (((y + step + 4) % 4) * 2 + z_lo) * 2 + core)
        return (((h + step + 4) % 4) * 4 + x, me)

    load_tok = pltpu.make_async_copy(tok_in, tok, lsem.at[4])
    load_cot = pltpu.make_async_copy(cot_in, cot, lsem.at[5])
    load_gate = pltpu.make_async_copy(gate_in, gate, lsem.at[0])
    load_down = pltpu.make_async_copy(down_in, down, lsem.at[1])
    half = pl.multiple_of(core * (D // 2), 128)
    load_raw = pltpu.make_async_copy(
        tok_in.at[:, pl.ds(pl.multiple_of(half + y * 384, 128), 384)],
        raw.at[0, 0, 0, pl.ds(0, TOK)],
        lsem.at[6 + 2 * NCH],
    )
    load_raw.start()
    load_tok.start()
    load_cot.start()
    load_gate.start()
    load_down.start()

    barrier = pltpu.get_barrier_semaphore()
    for axis in ("x", "z"):
        for step in (1, -1):
            pl.semaphore_signal(barrier, inc=1, device_id=peer(axis, step), device_id_type=MESH)

    def greet(i, carry):
        pl.semaphore_signal(barrier, inc=1, device_id=(dp, (me + i) % NE), device_id_type=MESH)
        return carry

    lax.fori_loop(1, NE, greet, 0)

    r = routes[...]
    w = wts[...]
    row16 = lax.broadcasted_iota(jnp.int32, (NE, TOK), 0)
    member = jnp.zeros((NE, TOK), F32)
    w_e = jnp.zeros((1, TOK), F32)
    for k in range(4):
        member = member + jnp.where(r[k : k + 1] == row16, 1.0, 0.0)
        w_e = w_e + jnp.where(r[k : k + 1] == me, w[k : k + 1], 0.0)
    before = lax.broadcasted_iota(jnp.int32, (TOK, TOK), 0) < lax.broadcasted_iota(
        jnp.int32, (TOK, TOK), 1
    )
    pos = jnp.dot(
        member.astype(BF), jnp.where(before, 1.0, 0.0).astype(BF), preferred_element_type=F32
    )
    slots = lax.broadcasted_iota(jnp.int32, (CAP, TOK), 0).astype(F32)

    def select(expert):
        mine = jnp.where(row16 == expert, 1.0, 0.0)
        mem_e = jnp.sum(member * mine, axis=0, keepdims=True)
        pos_e = jnp.sum(pos * mine, axis=0, keepdims=True)
        return jnp.where((pos_e == slots) & (mem_e > 0.5), 1.0, 0.0)

    sel = select(me)
    scale = jnp.sum(sel * w_e, axis=1, keepdims=True)
    scale_s[...] = jnp.broadcast_to(scale, (CAP, 128))
    sel_b = sel.astype(BF)
    pair = jnp.concatenate([sel, select(slot * 2 + 1 - core)], axis=0).astype(BF)
    for i in range(3):
        raw[0, 0, 0, TOK : TOK + 32, 128 * i : 128 * (i + 1)] = pair[32 * i : 32 * (i + 1)]
    load_raw.wait()
    pl.semaphore_wait(barrier, 4 + NE - 1)

    started = []
    count = [0]

    def remote(src, dst, device):
        i = count[0]
        count[0] += 1
        copy = pltpu.make_async_remote_copy(
            src_ref=src, dst_ref=dst, send_sem=ssem.at[i], recv_sem=rsem.at[i],
            device_id=device, device_id_type=MESH,
        )
        return copy

    def go(copy):
        copy.start()
        started.append(copy)

    class Gather:
        def __init__(self, axis, at):
            self.plus, self.minus = peer(axis, 1), peer(axis, -1)
            self.at = at
            self.p, self.m, self.f = {}, {}, {}
            for arr in (0, 1):
                self.p[arr] = remote(at(0, arr), at(3, arr), self.plus)
                self.m[arr] = remote(at(0, arr), at(1, arr), self.minus)
            self.f[0] = remote(at(3, 0), at(2, 0), self.plus)
            self.f[1] = remote(at(1, 1), at(2, 1), self.minus)

        def start(self, arr):
            first, second = (self.p, self.m) if arr == 0 else (self.m, self.p)
            go(first[arr])
            go(second[arr])

        def fwd(self, arr):
            (self.p if arr == 0 else self.m)[arr].wait_recv()
            go(self.f[arr])

        def near(self, arr):
            (self.m if arr == 0 else self.p)[arr].wait_recv()

        def far(self, arr):
            self.f[arr].wait_recv()

    CHUNKS = tuple(zip(EDGES[:-1], EDGES[1:]))
    def cut(i):
        return pl.ds(i * (GA // 2), GA // 2)

    def rest(i):
        return pl.ds(GA + i * ((D - GA) // 2), (D - GA) // 2)

    def piece(i):
        return pl.ds(i * 80, 80)

    a1 = Gather("z", lambda i, part: gat.at[i, 0, 1, :, cut(part)])
    a2 = [
        Gather("x", functools.partial(lambda u, i, part: gat.at[u, i, 1, :, cut(part)], u))
        for u in range(4)
    ]
    def sides(g):
        return slice(1, 3) if g == "s" else (0 if g == 0 else 3)

    b1 = Gather("x", lambda i, part: gat.at[0, i, 1, :, rest(part)])
    b2 = [
        Gather("z", functools.partial(lambda u, i, part: gat.at[i, u, 1, :, rest(part)], u))
        for u in range(4)
    ]
    c1 = Gather("z", lambda i, part: raw.at[0, POS[i], 0, piece(part)])
    c2 = {
        g: Gather("x", functools.partial(lambda g, i, part: raw.at[0, sides(g), POS[i], piece(part)], g))
        for g in (0, "s", 2)
    }
    cy = {
        (u, v): Gather(
            "y",
            functools.partial(
                lambda u, v, i, part: raw.at[i, sides(u), sides(v), pl.ds(64 * part, 64)], u, v
            ),
        )
        for u in (0, "s", 2)
        for v in (0, "s", 2)
        if (u, v) != (0, 0)
    }

    def sibling(u, v):
        return pltpu.make_async_remote_copy(
            src_ref=twin.at[u, v], dst_ref=gat.at[u, v, 0, :, pl.ds(half, D // 2)],
            send_sem=ts.at[4 * u + v], recv_sem=tr.at[4 * u + v],
            device_id=(dp, slot * 2 + 1 - core), device_id_type=MESH,
        )

    def from_sibling(u, v):
        other = pl.multiple_of((1 - core) * (D // 2), 128)
        return pltpu.make_async_remote_copy(
            src_ref=twin.at[u, v], dst_ref=gat.at[u, v, 0, :, pl.ds(other, D // 2)],
            send_sem=ts.at[4 * u + v], recv_sem=tr.at[4 * u + v],
            device_id=(dp, slot * 2 + 1 - core), device_id_type=MESH,
        )

    def pick(u, v):
        both = jnp.concatenate(
            [raw[0, POS[u], POS[v], TOK : TOK + 32, 128 * i : 128 * (i + 1)] for i in range(3)], axis=0
        )
        for r in range(4):
            res = jnp.dot(both, raw[r, POS[u], POS[v], :TOK], preferred_element_type=F32).astype(BF)
            c = ((y + r) % 4) * 384
            gat[u, v, 0, :, pl.ds(pl.multiple_of(half + c, 128), 384)] = res[:CAP]
            twin[u, v, :, pl.ds(pl.multiple_of(c, 128), 384)] = res[CAP:]
        sibling(u, v).start()

    def token_rows(u):
        for v in range(4):
            if (u, v) != (0, 0):
                from_sibling(u, v).wait_recv()

    def finish(ring):
        ring.near(0)
        ring.near(1)
        ring.far(0)
        ring.far(1)

    def rows(ref):
        return ref.reshape(4 * CAP, ref.shape[-1])

    def batch(u):
        t = rows(gat[u, :, 0])
        pre = jnp.dot(t, gate[...], preferred_element_type=F32)
        back = lax.dot_general(
            rows(gat[u, :, 1]), down[...], (((1,), (1,)), ((), ())), preferred_element_type=F32
        )
        s = jax.nn.sigmoid(pre)
        act = (pre * s).astype(BF)
        gp = (back * s * (1.0 + pre * (1.0 - s))).astype(BF)
        act_s[u] = act
        gp_s[u] = gp

        def cols(j, carry):
            c = pl.ds(pl.multiple_of(j * 512, 512), 512)
            o = jnp.dot(act_s[u], down[:, c], preferred_element_type=F32).astype(BF)
            par[u, :, 0, :, c] = o.reshape(4, CAP, 512)
            b = lax.dot_general(
                gp_s[u], gate[c, :], (((1,), (1,)), ((), ())), preferred_element_type=F32
            ).astype(BF)
            par[u, :, 1, :, c] = b.reshape(4, CAP, 512)
            return carry

        lax.fori_loop(0, D // 512, cols, 0)

    def drain(upto):
        for copy in started[:upto]:
            if copy is not None:
                copy.wait_send()
        started[:upto] = [None] * upto
    class Reduce:
        def __init__(self, axis, at, land, c):
            plus, minus = peer(axis, 1), peer(axis, -1)
            self.at, self.land, self.c = at, land, c
            self.f0 = remote(at(2, 0), land(0, 0), plus)
            self.f1 = remote(at(2, 1), land(0, 1), minus)
            self.l1 = remote(at(1, 1), land(1, 1), plus)
            self.r0 = remote(at(3, 0), land(2, 0), minus)
            self.l0 = remote(at(1, 0), land(1, 0), plus)
            self.r1 = remote(at(3, 1), land(2, 1), minus)

        def start(self):
            go(self.f0)
            go(self.f1)
            go(self.l1)
            go(self.r0)

        def fwd(self):
            for f, copy, i, arr in ((self.f0, self.l0, 1, 0), (self.f1, self.r1, 3, 1)):
                f.wait_recv()
                dst = self.at(i, arr)
                dst[...] = (dst[...].astype(F32) + self.land(0, arr)[...].astype(F32)).astype(BF)
                go(copy)

        def total(self, arr):
            return (
                self.at(0, arr)[...].astype(F32)
                + self.land(1, arr)[...].astype(F32)
                + self.land(2, arr)[...].astype(F32)
            )

        def arrive(self):
            for copy in (self.l1, self.r0, self.l0, self.r1):
                copy.wait_recv()

        def fin(self):
            self.arrive()
            for arr in (0, 1):
                self.at(0, arr)[...] = self.total(arr).astype(BF)

    def stage1(axis, u, c):
        if axis == "x":
            at = lambda i, arr: par.at[u, i, arr, :, c]
        else:
            at = lambda i, arr: par.at[i, u, arr, :, c]
        return Reduce(axis, at, lambda kind, arr: rd1.at[u, kind, arr, :, c], c)

    def stage2(axis, c):
        if axis == "x":
            at = lambda i, arr: par.at[0, i, arr, :, c]
        else:
            at = lambda i, arr: par.at[i, 0, arr, :, c]
        return Reduce(axis, at, lambda kind, arr: rd2.at[kind, arr, :, c], c)

    order = (0, 1, 3, 2)
    every = (slice(None),)
    first = [
        [stage1("x", u, pl.ds(lo, hi - lo)) for u in (every if lo else order)] for lo, hi in CHUNKS
    ]
    second = [stage2("z", pl.ds(lo, hi - lo)) for lo, hi in CHUNKS]
    rb = pl.ds(RA, D - RA)
    if RA < D:
        first_b = [stage1("z", u, rb) for u in every]
        second_b = stage2("x", rb)
    else:
        first_b = []

    def home(ring, lo, hi):
        ring.arrive()
        for arr in (0, 1):
            v = ring.total(arr)
            if arr == 0:
                v = v * scale_s[:, :1]
            v = v.astype(BF)
            for i in range((hi - lo) // 128):
                tile = lo // 128 + i
                ex[tile // 8, arr, tile % 8] = v[:, 128 * i : 128 * (i + 1)]

    def exchange(k, e_to, e_from):
        return pltpu.make_async_remote_copy(
            src_ref=ex.at[k, e_to % 2, e_to // 2], dst_ref=rx.at[k, e_from],
            send_sem=xs.at[k, e_to], recv_sem=xr.at[k, e_from],
            device_id=(dp, e_to), device_id_type=MESH,
        )

    def exchange_start(k):
        def one(i, carry):
            exchange(k, (me + i) % NE, me).start()
            return carry

        lax.fori_loop(1, NE, one, 0)
        rx[k, me] = ex[k, core, slot]

    def tile(k, owner):
        return pl.ds(pl.multiple_of(k * 1024 + owner * 128, 128), 128)

    def spread(k, to, frm):
        place = full.at[core, :, tile(k, frm)]
        return pltpu.make_async_remote_copy(
            src_ref=place, dst_ref=place,
            send_sem=os_.at[k, to], recv_sem=or_.at[k, frm],
            device_id=(dp, to * 2 + core), device_id_type=MESH,
        )

    def mix(k):
        def one(i, carry):
            exchange(k, me, (me + i) % NE).wait_recv()
            return carry

        lax.fori_loop(1, NE, one, 0)
        full[core, :, tile(k, slot)] = lax.dot_general(
            sel_s[...], rx[k].reshape(NE * CAP, 128), (((0,), (0,)), ((), ())),
            preferred_element_type=F32,
        ).astype(BF)

        def two(i, carry):
            spread(k, (slot + i) % 8, slot).start()
            return carry

        lax.fori_loop(1, 8, two, 0)

    def relay(k):
        place = full.at[core, :, 1024 * k : 1024 * (k + 1)]
        return pltpu.make_async_remote_copy(
            src_ref=place, dst_ref=place, send_sem=ks.at[k], recv_sem=kr.at[k],
            device_id=(dp, slot * 2 + 1 - core), device_id_type=MESH,
        )

    def keep(k, arr):
        cols = slice(1024 * k, 1024 * (k + 1))
        return pltpu.make_async_copy(
            full.at[arr, :, cols], (mixed, tgrad)[arr].at[:, cols], lsem.at[6 + 2 * k + arr]
        )

    def relay_start(k):
        def one(i, carry):
            spread(k, slot, (slot + i) % 8).wait_recv()
            return carry

        lax.fori_loop(1, 8, one, 0)
        relay(k).start()

    def relay_finish(k):
        other = full.at[1 - core, :, 1024 * k : 1024 * (k + 1)]
        pltpu.make_async_remote_copy(
            src_ref=other, dst_ref=other, send_sem=ks.at[k], recv_sem=kr.at[k],
            device_id=(dp, slot * 2 + 1 - core), device_id_type=MESH,
        ).wait_recv()
        keep(k, 0).start()
        keep(k, 1).start()

    def grads(j):
        c = pl.ds(512 * j, 512)
        t = gat[:, :, 0, :, c].reshape(NE * CAP, 512)
        g = gat[:, :, 1, :, c].reshape(NE * CAP, 512)
        dg[:, c] = lax.dot_general(
            act_s[...].reshape(NE * CAP, HID), g, (((0,), (0,)), ((), ())),
            preferred_element_type=F32,
        ).astype(BF)
        gg[c, :] = lax.dot_general(
            t, gp_s[...].reshape(NE * CAP, HID), (((0,), (0,)), ((), ())),
            preferred_element_type=F32,
        ).astype(BF)

    def drain(upto):
        for copy in started[:upto]:
            if copy is not None:
                copy.wait_send()
        started[:upto] = [None] * upto

    def both(f):
        f(0)
        f(1)

    def begin(ring):
        both(ring.start)

    def onward(ring):
        both(ring.fwd)

    both(c1.start)
    begin(c2[0])
    load_cot.wait()
    gat[0, 0, 1] = (jnp.dot(sel_b, cot[...], preferred_element_type=F32) * scale).astype(BF)
    begin(b1)
    begin(a2[0])
    load_tok.wait()
    gat[0, 0, 0] = jnp.dot(sel_b, tok[...], preferred_element_type=F32).astype(BF)
    onward(c2[0])
    both(c2[0].near)
    begin(cy[0, "s"])
    onward(c1)
    both(a1.start)
    both(c1.near)
    begin(c2["s"])
    begin(cy["s", 0])
    both(c2[0].far)
    begin(cy[0, 2])
    both(c1.far)
    begin(c2[2])
    onward(cy[0, "s"])
    onward(b1)
    begin(b2[0])
    onward(a2[0])
    onward(c2["s"])
    onward(cy["s", 0])
    onward(cy[0, 2])
    both(c2["s"].near)
    begin(cy["s", "s"])
    a1.fwd(0)
    a2[3].start(0)
    a1.fwd(1)
    a2[1].start(1)
    a1.near(0)
    a2[1].start(0)
    a1.near(1)
    a2[3].start(1)
    finish(cy[0, "s"])
    pick(0, 1)
    pick(0, 3)
    onward(c2[2])
    finish(cy[0, 2])
    pick(0, 2)
    a2[3].fwd(0)
    a2[1].fwd(1)
    both(c2["s"].far)
    begin(cy["s", 2])
    a1.far(0)
    a2[2].start(0)
    a1.far(1)
    a2[2].start(1)
    both(b1.near)
    begin(b2[1])
    begin(b2[3])
    onward(b2[0])
    both(b1.far)
    begin(b2[2])
    onward(cy["s", "s"])
    finish(cy["s", 0])
    pick(1, 0)
    pick(3, 0)
    a2[1].fwd(0)
    a2[3].fwd(1)
    onward(cy["s", 2])
    onward(b2[1])
    onward(b2[3])
    both(c2[2].near)
    begin(cy[2, 0])
    begin(cy[2, "s"])
    finish(a2[0])
    load_gate.wait()
    load_down.wait()
    token_rows(0)
    batch(0)
    finish(cy["s", "s"])
    pick(1, 1)
    pick(1, 3)
    both(c2[2].far)
    begin(cy[2, 2])
    pick(3, 1)
    pick(3, 3)
    onward(b2[2])
    a2[2].fwd(0)
    a2[2].fwd(1)
    finish(cy["s", 2])
    pick(1, 2)
    pick(3, 2)
    onward(cy[2, 0])
    onward(cy[2, "s"])
    for ring in b2:
        both(ring.near)
    finish(a2[1])
    token_rows(1)
    batch(1)
    first[0][0].start()
    onward(cy[2, 2])
    finish(cy[2, 0])
    pick(2, 0)
    finish(a2[3])
    token_rows(3)
    batch(3)
    first[0][1].start()
    first[0][2].start()
    finish(cy[2, "s"])
    pick(2, 1)
    pick(2, 3)
    finish(cy[2, 2])
    pick(2, 2)
    for ring in b2:
        both(ring.far)
    finish(a2[2])
    token_rows(2)
    batch(2)
    first[0][3].start()
    for ring in first_b:
        ring.start()
    for e in range(NE):
        sel_s[CAP * e : CAP * (e + 1), :] = jnp.where(
            (pos[e : e + 1] == slots) & (member[e : e + 1] > 0.5), 1.0, 0.0
        ).astype(BF)

    n = len(CHUNKS)
    ready = []
    todo = []

    def came(k):
        home(second[k], *CHUNKS[k])
        hi = CHUNKS[k][1]
        if hi in (1024, 2048, RA):
            g = {1024: 0, 2048: 1, RA: 2}[hi]
            if g == 2:
                if RA < D:
                    home(second_b, RA, D)
            exchange_start(g)
            todo.append([g, 0])

    def advance():
        for item in todo:
            g, state = item
            if state < 3:
                (mix, relay_start, relay_finish)[state](g)
                item[1] += 1

    for k in range(n):
        mark = len(started)
        for i, ring in enumerate(first[k]):
            ring.fwd()
            if k == 0:
                grads(i)
            if k + 1 < n and i == 0:
                first[k + 1][0].start()
        if k == 1:
            for ring in first_b:
                ring.fwd()
        if k == 0:
            grads(4)
            grads(5)
        if k >= 1:
            second[k - 1].fwd()
        if k >= 2:
            advance()
            came(k - 2)
            drain(old)
        old = mark
        for ring in first[k]:
            ring.fin()
        second[k].start()
        if k == 2 and RA < D:
            for ring in first_b:
                ring.fin()
            second_b.start()
        if k == 3 and RA < D:
            second_b.fwd()
    came(n - 2)
    second[n - 1].fwd()
    came(n - 1)
    mix(1)
    relay_finish(0)
    mix(2)
    relay_start(1)
    drain(old)
    relay_start(2)
    relay_finish(1)
    relay_finish(2)

    for k in range(NCH):
        keep(k, 0).wait()
        keep(k, 1).wait()
        relay(k).wait_send()

        def last(i, carry, k=k):
            exchange(k, (me + i) % NE, me).wait_send()
            return carry

        lax.fori_loop(1, NE, last, 0)

        def last_spread(i, carry, k=k):
            spread(k, (slot + i) % 8, slot).wait_send()
            return carry

        lax.fori_loop(1, 8, last_spread, 0)
    for u in range(4):
        for v in range(4):
            if (u, v) != (0, 0):
                sibling(u, v).wait_send()
    drain(len(started))


N_COPY = 10 * 6 + 5 * 6 * len(EDGES)


def shards(tokens, cotangent, routes, route_weights, gate_weight, down_weight):
    gate_weight = gate_weight.reshape(D, HID)
    down_weight = down_weight.reshape(HID, D)
    mixed, tgrad, gg, dg = pl.pallas_call(
        kernel,
        out_shape=(
            pltpu.VMEM((TOK, D), BF),
            pltpu.VMEM((TOK, D), BF),
            pltpu.VMEM((D, HID), BF),
            pltpu.VMEM((HID, D), BF),
        ),
        in_specs=[HB, HB, VM, VM, HB, HB],
        out_specs=(VM, VM, VM, VM),
        scratch_shapes=[
            pltpu.VMEM((TOK, D), BF),
            pltpu.VMEM((TOK, D), BF),
            pltpu.VMEM((4, 4, 4, TOK + 32, 384), BF),
            pltpu.VMEM((4, 4, CAP, D // 2), BF),
            pltpu.VMEM((4, 4, 2, CAP, D), BF),
            pltpu.VMEM((4, 4, 2, CAP, D), BF),
            pltpu.VMEM((4, 3, 2, CAP, D), BF),
            pltpu.VMEM((3, 2, CAP, D), BF),
            pltpu.VMEM((D, HID), BF),
            pltpu.VMEM((HID, D), BF),
            pltpu.VMEM((4, 4 * CAP, HID), BF),
            pltpu.VMEM((4, 4 * CAP, HID), BF),
            pltpu.VMEM((NCH, 2, 8, CAP, 128), BF),
            pltpu.VMEM((NCH, NE, CAP, 128), BF),
            pltpu.VMEM((2, TOK, D), BF),
            pltpu.VMEM((NE * CAP, TOK), BF),
            pltpu.VMEM((CAP, 128), F32),
            pltpu.SemaphoreType.DMA((15 * 6 + 15 * 6 + 5 * 6 * len(EDGES),)),
            pltpu.SemaphoreType.DMA((15 * 6 + 15 * 6 + 5 * 6 * len(EDGES),)),
            pltpu.SemaphoreType.DMA((NCH, NE)),
            pltpu.SemaphoreType.DMA((NCH, NE)),
            pltpu.SemaphoreType.DMA((NCH, 8)),
            pltpu.SemaphoreType.DMA((NCH, 8)),
            pltpu.SemaphoreType.DMA((NCH,)),
            pltpu.SemaphoreType.DMA((NCH,)),
            pltpu.SemaphoreType.DMA((16,)),
            pltpu.SemaphoreType.DMA((16,)),
            pltpu.SemaphoreType.DMA((7 + 2 * NCH,)),
        ],
        compiler_params=pltpu.CompilerParams(
            collective_id=0, has_side_effects=True, vmem_limit_bytes=56 * 2**20
        ),
        cost_estimate=pl.CostEstimate(
            flops=12 * 768 * D * HID, bytes_accessed=2 * 10**7, transcendentals=768 * HID
        ),
        name="moe",
    )(tokens, cotangent, routes.T, route_weights.T, gate_weight, down_weight)
    return mixed, tgrad, gg.reshape(1, D, HID), dg.reshape(1, HID, D)


def solution(mesh):
    return jax.shard_map(
        shards,
        mesh=mesh,
        in_specs=(
            P("dp", None),
            P("dp", None),
            P("dp", None),
            P("dp", None),
            P("expert", None, "dp"),
            P("expert", "dp", None),
        ),
        out_specs=(P("dp", None), P("dp", None), P("expert", None, "dp"), P("expert", "dp", None)),
        check_vma=False,
    )
```
